32 devices in a mesh: dp: 8 (over z, y), mp: 4 (over x, core).
Axes of the slice: x: 2, y: 2, z: 4, core: 2. Of those that a mesh axis runs over, the one named last changes fastest.
Arguments:
- tokens: bfloat16 [2048, 4096], P('dp', 'mp'), may hold values from -24 to 24
- cotangent: bfloat16 [2048, 4096], P('dp', 'mp'), may hold values from -6 to 6
- gain_dec: float32 [4096], replicated, may hold values from 0.1 to 1.9
- w_query: bfloat16 [4096, 4096], P(None, 'mp'), may hold values from -1 to 1
- w_out: bfloat16 [4096, 4096], P('mp'), may hold values from -0.5 to 0.5
- encodings: bfloat16 [64, 128, 896], P('dp', 'mp'), may hold values from -24 to 24
- gain_enc: float32 [896], replicated, may hold values from 0.1 to 1.9
- w_key: bfloat16 [896, 4096], P(None, 'mp'), may hold values from -1 to 1
- w_value: bfloat16 [896, 4096], P(None, 'mp'), may hold values from -0.1875 to 0.1875
- gain_post: float32 [4096], replicated, may hold values from 0.1 to 1.9
- neighbour_ids: int32 [32, 2], P('dp'), may hold values from 0 to 63, as said below
Outputs:
- mixed: bfloat16 [2048, 4096], P('dp', 'mp')
- ffn_input: bfloat16 [2048, 4096], P('dp', 'mp')
- d_encodings: bfloat16 [64, 128, 896], P('dp', 'mp')
The draws below stay inside these ranges and needn't reach their ends.
Inputs may be any that keep to these rules, and one draw needn't show every extreme that they name: `neighbour_ids`: encoder row g is held by index g // 8 of dp. Every encoder row is retrieved by exactly one block. The blocks of one index of dp retrieve at most 1 row held by any one index of dp, and exactly 1 from some.
All inputs are finite; a program needn't handle non-finite values.
Results may differ from the reference program's by a relative error of at most 0.02.
The reference program's roundings to bfloat16 on the way count: a program that leaves them out, or rounds other values in their place, can miss the bound.
Values may be sent and summed in bfloat16 or wider, within the bound.
A program may use at most 64 MiB of HBM per device.

```python
import math
import jax
import jax.numpy as jnp
from jax import lax

D = 4096
HEADS = 32
HD = 128
EW = 896
BLOCK = 64
NLEN = 128
NEIGH = 2
TOK_DEV = 256
BLOCKS_DEV = 4
REFS = 8
TOKENS = 2048
ROWS = 64
N_DP = 8
N_MP = 4


def scaled_field(key, shape):
    k_base, k_rows, k_cols = jax.random.split(key, 3)
    base = jnp.clip(jax.random.normal(k_base, shape, jnp.float32), -4.0, 4.0)
    row_scale = jnp.exp(jax.random.uniform(k_rows, shape[:-1] + (1,), jnp.float32, math.log(0.3), math.log(3.0)))
    col_scale = jnp.exp(jax.random.uniform(k_cols, (shape[-1],), jnp.float32, math.log(0.5), math.log(2.0)))
    return base * row_scale * col_scale


def draw_tokens(key, part):
    return scaled_field(jax.random.fold_in(key, 1), (TOKENS, D)).astype(jnp.bfloat16)


def draw_encodings(key, part):
    return scaled_field(jax.random.fold_in(key, 2), (ROWS, NLEN, EW)).astype(jnp.bfloat16)


def draw_w_query(key, part):
    base = jnp.clip(jax.random.normal(jax.random.fold_in(key, 3), (D, HEADS * HD), jnp.float32), -4.0, 4.0) / math.sqrt(D)
    return jnp.clip(base, -1.0, 1.0).astype(jnp.bfloat16)


def draw_w_key(key, part):
    base = jnp.clip(jax.random.normal(jax.random.fold_in(key, 5), (EW, HEADS * HD), jnp.float32), -4.0, 4.0) / math.sqrt(EW)
    return jnp.clip(base, -1.0, 1.0).astype(jnp.bfloat16)


def draw_neighbour_ids(key, part):
    k_shift, k_own, k_read = jax.random.split(jax.random.fold_in(key, 9), 3)
    spread = min(N_DP, REFS)
    shuffled = jax.random.permutation(k_shift, N_DP).astype(jnp.int32)
    places = jnp.arange(N_DP, dtype=jnp.int32)
    front = jnp.where(shuffled == 1, 0, jnp.where(shuffled == N_DP // 2, 1, jnp.where(shuffled == N_DP - 1, 2, 3 + places)))
    shuffled = shuffled[jnp.argsort(front).astype(jnp.int32)]
    shifts = shuffled[jnp.arange(REFS, dtype=jnp.int32) % spread]
    owners = jnp.arange(N_DP, dtype=jnp.int32)
    targets = (owners[:, None] + shifts[None, :]) % N_DP
    row_perm = jax.vmap(lambda subkey: jax.random.permutation(subkey, REFS))(jax.random.split(k_own, N_DP))
    targets = jnp.take_along_axis(targets, row_perm.astype(jnp.int32), axis=1)
    flat_targets = targets.reshape(N_DP * REFS)
    row_ids = jnp.arange(N_DP * REFS, dtype=jnp.int32)
    by_reader = jnp.argsort(flat_targets * (N_DP * REFS) + row_ids).astype(jnp.int32).reshape(N_DP, REFS)
    read_perm = jax.vmap(lambda subkey: jax.random.permutation(subkey, REFS))(jax.random.split(k_read, N_DP))
    chosen = jnp.take_along_axis(by_reader, read_perm.astype(jnp.int32), axis=1)
    return chosen.reshape(N_DP * BLOCKS_DEV, NEIGH)


def block_scale(own_key, extent, shards, low, high):
    factor_of = 1.0
    for position, shards_of in shards:
        steps = jax.random.uniform(jax.random.fold_in(jax.random.fold_in(own_key, 6), position), (shards_of,), jnp.float32, low / len(shards), high / len(shards))
        factor_of = factor_of * jnp.repeat(jnp.exp(steps), extent[position] // shards_of).reshape((-1,) + (1,) * (len(extent) - 1 - position))
    return factor_of


def normal_values(key, dims, deviation, limit, cuts=(), held_as=jnp.bfloat16):
    loudness = block_scale(key, dims, cuts, -0.22, 0.18) if cuts else 1.0
    entries = jax.random.normal(key, dims, jnp.float32) * deviation * loudness
    return jnp.minimum(jnp.maximum(entries, -limit), limit).astype(held_as)


def setup_inputs(seed: int = 0) -> dict:
    streams_of = jax.random.split(jax.random.key(seed), 12)
    return {
        "tokens": draw_tokens(jax.random.fold_in(streams_of[11], 71), 0),
        "cotangent": normal_values(streams_of[1], (TOKENS, D), 1.0, 6.0, ((0, 8), (1, 4))),
        "gain_dec": jnp.clip(1.0 + 0.18 * jax.random.normal(streams_of[2], (D,), jnp.float32), 0.1, 1.9),
        "w_query": draw_w_query(jax.random.fold_in(streams_of[11], 71), 0),
        "w_out": normal_values(streams_of[4], (HEADS * HD, D), (HEADS * HD // 32) ** -0.5, 0.5, ((0, 4),)),
        "encodings": draw_encodings(jax.random.fold_in(streams_of[11], 71), 0),
        "gain_enc": jnp.clip(1.0 + 0.18 * jax.random.normal(streams_of[6], (EW,), jnp.float32), 0.1, 1.9),
        "w_key": draw_w_key(jax.random.fold_in(streams_of[11], 71), 0),
        "w_value": normal_values(streams_of[8], (EW, HEADS * HD), EW ** -0.5, 0.1875, ((1, 4),)),
        "gain_post": jnp.clip(1.0 + 0.18 * jax.random.normal(streams_of[9], (D,), jnp.float32), 0.1, 1.9),
        "neighbour_ids": draw_neighbour_ids(jax.random.fold_in(streams_of[11], 71), 0),
    }


EPS = 1e-06

def rms_scale(values):
    return lax.rsqrt(lax.optimization_barrier(jnp.mean(values * values, axis=-1, keepdims=True)) + EPS)

def rounded(values):
    return lax.optimization_barrier(values.astype(jnp.bfloat16)).astype(jnp.float32)

def reference(tokens, cotangent, gain_dec, w_query, w_out, encodings, gain_enc, w_key, w_value, gain_post, neighbour_ids):
    head_cols = HEADS * HD
    group_cols = head_cols // N_MP
    lead_in = BLOCK - 1
    score_scale = HD ** (-0.5)
    enc_wide = encodings.astype(jnp.float32)
    row_scale = rms_scale(enc_wide)
    normed_enc = (enc_wide * row_scale * gain_enc).astype(jnp.bfloat16)
    key_weights = w_key.astype(jnp.float32)
    value_weights = w_value.astype(jnp.float32)
    out_groups = w_out.astype(jnp.float32).reshape(N_MP, group_cols, D)
    key_groups = key_weights.reshape(EW, N_MP, group_cols)
    value_groups = value_weights.reshape(EW, N_MP, group_cols)

    def one_sequence(seq):
        rows_in = lax.dynamic_slice_in_dim(tokens, seq * TOK_DEV, TOK_DEV, 0)
        rows_grad = lax.dynamic_slice_in_dim(cotangent, seq * TOK_DEV, TOK_DEV, 0)
        chosen = lax.dynamic_slice_in_dim(neighbour_ids, seq * BLOCKS_DEV, BLOCKS_DEV, 0).reshape(REFS)
        tok_wide = rows_in.astype(jnp.float32)
        normed = (tok_wide * rms_scale(tok_wide) * gain_dec).astype(jnp.bfloat16)
        queries = rounded(jnp.dot(normed, w_query, preferred_element_type=jnp.float32))
        memory = normed_enc[chosen].astype(jnp.float32)
        key_rows = rounded(jnp.einsum('ate,ej->atj', memory, key_weights))
        value_rows = rounded(jnp.einsum('ate,ej->atj', memory, value_weights))
        key_blocks = key_rows.reshape(BLOCKS_DEV, NEIGH * NLEN, HEADS, HD)
        value_blocks = value_rows.reshape(BLOCKS_DEV, NEIGH * NLEN, HEADS, HD)
        shifted = jnp.concatenate([queries[lead_in:], jnp.zeros((lead_in, head_cols), jnp.float32)], axis=0)
        shifted = shifted.reshape(BLOCKS_DEV, BLOCK, HEADS, HD)
        scores = jnp.einsum('cqhd,ckhd->chqk', shifted, key_blocks) * score_scale
        probability = jax.nn.softmax(scores, axis=-1)
        weights = rounded(probability)
        attended = rounded(jnp.einsum('chqk,ckhd->cqhd', weights, value_blocks)).reshape(TOK_DEV, head_cols)
        attended = jnp.concatenate([jnp.zeros((lead_in, head_cols), jnp.float32), attended[:TOK_DEV - lead_in]], axis=0)
        branch = rounded(jnp.einsum('tgj,gjd->tgd', attended.reshape(TOK_DEV, N_MP, group_cols), out_groups))
        mixed = (tok_wide + lax.optimization_barrier(jnp.sum(branch, axis=1))).astype(jnp.bfloat16)
        mixed_wide = mixed.astype(jnp.float32)
        ffn_input = (mixed_wide * rms_scale(mixed_wide) * gain_post).astype(jnp.bfloat16)
        d_attended = rounded(jnp.dot(rows_grad, w_out.T, preferred_element_type=jnp.float32))
        d_shifted = jnp.concatenate([d_attended[lead_in:], jnp.zeros((lead_in, head_cols), jnp.float32)], axis=0)
        d_shifted = d_shifted.reshape(BLOCKS_DEV, BLOCK, HEADS, HD)
        value_grad = rounded(jnp.einsum('chqk,cqhd->ckhd', weights, d_shifted))
        d_probability = jnp.einsum('cqhd,ckhd->chqk', d_shifted, value_blocks)
        d_scores = rounded(probability * (d_probability - lax.optimization_barrier(jnp.sum(probability * d_probability, axis=-1, keepdims=True))) * score_scale)
        key_grad = rounded(jnp.einsum('chqk,cqhd->ckhd', d_scores, shifted))
        key_parts = key_grad.reshape(REFS, NLEN, N_MP, group_cols)
        value_parts = value_grad.reshape(REFS, NLEN, N_MP, group_cols)
        terms = rounded(jnp.einsum('atgj,egj->atge', key_parts, key_groups) + jnp.einsum('atgj,egj->atge', value_parts, value_groups))
        return (mixed, ffn_input, lax.optimization_barrier(jnp.sum(terms, axis=2)), chosen)
    mixed, ffn_input, d_normed, chosen = lax.map(one_sequence, jnp.arange(N_DP, dtype=jnp.int32))
    mixed = mixed.reshape(TOKENS, D)
    ffn_input = ffn_input.reshape(TOKENS, D)
    grad_rows = jnp.zeros((ROWS, NLEN, EW), jnp.float32).at[chosen.reshape(ROWS)].add(d_normed.reshape(ROWS, NLEN, EW))
    enc_hat = enc_wide * row_scale
    upstream = gain_enc * grad_rows
    d_encodings = (row_scale * (upstream - enc_hat * lax.optimization_barrier(jnp.mean(upstream * enc_hat, axis=-1, keepdims=True)))).astype(jnp.bfloat16)
    return (mixed, ffn_input, d_encodings)
```

```python
import functools

import jax
import jax.numpy as jnp
from jax import lax
from jax.experimental import pallas as pl
from jax.experimental.pallas import tpu as pltpu
from jax.sharding import PartitionSpec as P

HD = 128
BLOCK = 64
NLEN = 128
NEIGH = 2
LEAD = BLOCK - 1
EPS = 1e-06
MESH = pl.DeviceIdType.MESH
BF16 = jnp.bfloat16
F32 = jnp.float32
NT = (((1,), (1,)), ((), ()))
TN = (((0,), (0,)), ((), ()))


def rms_scale(values):
    return lax.rsqrt(jnp.mean(values * values, axis=-1, keepdims=True) + EPS)


def place(n_dp, n_mp):
    d, m = lax.axis_index("dp"), lax.axis_index("mp")
    n_x = n_mp // 2
    x, c = m // 2, m % 2
    return d, m, n_x, x, c, x * 2 + (1 - c)


def greet(n_dp, n_mp, d, m):
    barrier = pltpu.get_barrier_semaphore()
    for s in range(1, n_dp):
        pl.semaphore_signal(barrier, inc=1, device_id=((d + s) % n_dp, m), device_id_type=MESH)
    for s in range(1, n_mp):
        pl.semaphore_signal(barrier, inc=1, device_id=(d, (m + s) % n_mp), device_id_type=MESH)
    pl.semaphore_wait(barrier, n_dp + n_mp - 2)


def gather_kernel(
    n_dp, n_mp,
    tok, cot, gain_dec, wq_hbm, wo_hbm, enc, gain_enc, wk_hbm, wv_hbm, ids, owner,
    q_out, da_out, k_out, v_out, idtab,
    tok_all, cot_all, enc_all, normed, wq, wo, wk, wv, enc_norm, sending, arrived,
    w_sem, ag_send, ag_recv, id_send, id_recv, row_send, row_recv,
):
    d, m, n_x, x, c, partner = place(n_dp, n_mp)
    own_rows, share, width = enc.shape
    readings = ids.shape[0]
    seq_len, feat = tok.shape
    head_cols = wq.shape[2]
    loads = [
        pltpu.make_async_copy(a, b, w_sem.at[i])
        for i, (a, b) in enumerate([(wq_hbm, wq), (wo_hbm, wo), (wk_hbm, wk), (wv_hbm, wv)])
    ]
    for load in loads:
        load.start()

    def hop(buf, t, kind, chunk, target):
        return pltpu.make_async_remote_copy(
            src_ref=buf.at[chunk], dst_ref=buf.at[chunk],
            send_sem=ag_send.at[t, kind], recv_sem=ag_recv.at[t, kind],
            device_id=(d, target), device_id_type=MESH,
        )

    def spread(buf, t):
        for o in range(1, n_x):
            hop(buf, t, o, m, ((x + o) % n_x) * 2 + c).start()
        hop(buf, t, 0, m, partner).start()

    def forward(buf, t):
        for o in range(1, n_x):
            chunk = ((x + n_x - o) % n_x) * 2 + c
            hop(buf, t, o, chunk, partner).wait_recv()
            hop(buf, t, n_x + o, chunk, partner).start()

    def finish(buf, t):
        hop(buf, t, 0, partner, partner).wait_recv()
        for o in range(1, n_x):
            hop(buf, t, n_x + o, ((x + n_x - o) % n_x) * 2 + 1 - c, partner).wait_recv()

    def sent_far(buf, t):
        for o in range(1, n_x):
            hop(buf, t, o, m, partner).wait_send()

    def sent_near(buf, t):
        hop(buf, t, 0, m, partner).wait_send()
        for o in range(1, n_x):
            hop(buf, t, n_x + o, m, partner).wait_send()

    def id_copy(s, to):
        return pltpu.make_async_remote_copy(
            src_ref=ids, dst_ref=idtab.at[to], send_sem=id_send.at[s], recv_sem=id_recv.at[s],
            device_id=((d + s) % n_dp, m), device_id_type=MESH,
        )

    def row_copy(s, src, dst):
        return pltpu.make_async_remote_copy(
            src_ref=sending.at[src], dst_ref=arrived.at[dst],
            send_sem=row_send.at[s], recv_sem=row_recv.at[s],
            device_id=((d + s) % n_dp, m), device_id_type=MESH,
        )

    tok_all[m] = tok[...]
    greet(n_dp, n_mp, d, m)
    for s in range(1, n_dp):
        id_copy(s, d).start()
    spread(tok_all, 0)
    idtab[d] = ids[...]
    cot_all[m] = cot[...]
    wide = enc[...].astype(F32)
    enc_norm[...] = wide * rms_scale(wide) * gain_enc[...][None]

    def choose(reader):
        asked = idtab[reader]
        total = jnp.zeros((share, width), F32)
        for row in range(own_rows):
            hit = jnp.where(asked == d * own_rows + row, 1.0, 0.0).astype(F32)
            hit = jnp.max(hit, axis=0, keepdims=True)
            total = total + enc_norm[row] * jnp.concatenate([hit] * (width // 128), axis=1)
        return total.astype(BF16)

    arrived[d] = choose(d)
    for s in range(1, n_dp):
        reader = (d + s) % n_dp
        id_copy(n_dp - s, reader).wait_recv()
        sending[reader] = choose(reader)
        row_copy(s, reader, d).start()
    sent_far(tok_all, 0)
    spread(cot_all, 1)
    forward(tok_all, 0)
    for s in range(1, n_dp):
        holder = (d + n_dp - s) % n_dp
        row_copy(s, holder, holder).wait_recv()
    for a in range(readings):
        enc_all[m, a] = arrived[owner[a]]
    spread(enc_all, 2)
    finish(tok_all, 0)
    squares = jnp.zeros((seq_len, 1), F32)
    for k in range(n_mp):
        part = tok_all[k].astype(F32)
        squares = squares + jnp.sum(part * part, axis=-1, keepdims=True)
    scale = lax.rsqrt(squares / (feat * n_mp) + EPS)
    for k in range(n_mp):
        normed[k] = (tok_all[k].astype(F32) * scale * gain_dec[k]).astype(BF16)
    loads[0].wait()
    keep = lax.broadcasted_iota(jnp.int32, (seq_len, 256), 0) < seq_len - LEAD

    def shift_up(values):
        return jnp.where(keep, pltpu.roll(values, seq_len - LEAD, 0), 0.0).astype(BF16)

    def query_tile(n, _):
        cols = pl.ds(pl.multiple_of(n * 256, 256), 256)
        acc = jnp.zeros((seq_len, 256), F32)
        for k in range(n_mp):
            acc += jnp.dot(normed[k], wq[k, :, cols], preferred_element_type=F32)
        q_out[:, cols] = shift_up(acc)
        return 0

    lax.fori_loop(0, head_cols // 256, query_tile, 0)
    forward(cot_all, 1)
    finish(cot_all, 1)
    loads[1].wait()

    def grad_tile(n, _):
        cols = pl.ds(pl.multiple_of(n * 256, 256), 256)
        acc = jnp.zeros((seq_len, 256), F32)
        for k in range(n_mp):
            acc += lax.dot_general(
                cot_all[k], wo[cols, k * feat : (k + 1) * feat], NT, preferred_element_type=F32
            )
        da_out[:, cols] = shift_up(acc)
        return 0

    lax.fori_loop(0, head_cols // 256, grad_tile, 0)
    forward(enc_all, 2)
    finish(enc_all, 2)
    loads[2].wait()
    loads[3].wait()

    def memory_tile(n, _):
        cols = pl.ds(pl.multiple_of(n * 256, 256), 256)
        for k in range(n_mp):
            rows = enc_all[k].reshape(readings * share, width)
            for weight, out in ((wk, k_out), (wv, v_out)):
                part = jnp.dot(rows, weight[:, cols], preferred_element_type=F32).astype(BF16)
                out[:, k * share : (k + 1) * share, cols] = part.reshape(readings, share, 256)
        return 0

    lax.fori_loop(0, head_cols // 256, memory_tile, 0)
    for s in range(1, n_dp):
        id_copy(s, d).wait_send()
        row_copy(s, (d + s) % n_dp, d).wait_send()
    sent_far(cot_all, 1)
    sent_far(enc_all, 2)
    sent_near(tok_all, 0)
    sent_near(cot_all, 1)
    sent_near(enc_all, 2)


def attend_kernel(
    n_mp, q, da, keys, values, wk_hbm, wv_hbm, wo_hbm, enc_terms, branches,
    dk, dv, att, att16, wk, wv, wo, w_sem,
):
    loads = [
        pltpu.make_async_copy(a, b, w_sem.at[i])
        for i, (a, b) in enumerate([(wk_hbm, wk), (wv_hbm, wv), (wo_hbm, wo)])
    ]
    for load in loads:
        load.start()
    seq_len, head_cols = q.shape
    readings, _, width = dk.shape[0], dk.shape[1], wk.shape[0]
    share = NLEN // n_mp
    feat = wo.shape[1] // n_mp
    factor = HD ** (-0.5)

    def one_block(b, _):
        rows = pl.ds(pl.multiple_of(b * BLOCK, BLOCK), BLOCK)
        mem = pl.ds(b * NEIGH, NEIGH)
        for h in range(head_cols // HD):
            cols = slice(h * HD, (h + 1) * HD)
            q_h, da_h = q[rows, cols], da[rows, cols]
            k_h = keys[mem, :, cols].reshape(NEIGH * NLEN, HD)
            v_h = values[mem, :, cols].reshape(NEIGH * NLEN, HD)
            scores = lax.dot_general(q_h, k_h, NT, preferred_element_type=F32) * factor
            lifted = jnp.exp(scores - jnp.max(scores, axis=-1, keepdims=True))
            prob = lifted / jnp.sum(lifted, axis=-1, keepdims=True)
            weights = prob.astype(BF16)
            att[rows, cols] = jnp.dot(weights, v_h, preferred_element_type=F32)
            d_prob = lax.dot_general(da_h, v_h, NT, preferred_element_type=F32)
            inner = jnp.sum(prob * d_prob, axis=-1, keepdims=True)
            d_scores = (prob * (d_prob - inner) * factor).astype(BF16)
            dv_h = lax.dot_general(weights, da_h, TN, preferred_element_type=F32).astype(BF16)
            dk_h = lax.dot_general(d_scores, q_h, TN, preferred_element_type=F32).astype(BF16)
            dv[mem, :, cols] = dv_h.reshape(NEIGH, NLEN, HD)
            dk[mem, :, cols] = dk_h.reshape(NEIGH, NLEN, HD)
        return 0

    lax.fori_loop(0, seq_len // BLOCK, one_block, 0)
    low = lax.broadcasted_iota(jnp.int32, (seq_len, head_cols), 0) >= LEAD
    att16[...] = jnp.where(low, pltpu.roll(att[...], LEAD, 0), 0.0).astype(BF16)
    loads[0].wait()
    loads[1].wait()

    def enc_chunk(k, _):
        toks = pl.ds(pl.multiple_of(k * share, share), share)
        acc = lax.dot_general(
            dk[:, toks, :].reshape(readings * share, head_cols), wk[...], NT,
            preferred_element_type=F32,
        )
        acc += lax.dot_general(
            dv[:, toks, :].reshape(readings * share, head_cols), wv[...], NT,
            preferred_element_type=F32,
        )
        enc_terms[k] = acc.astype(BF16).reshape(readings, share, width)
        return 0

    lax.fori_loop(0, n_mp, enc_chunk, 0)
    loads[2].wait()

    def branch_chunk(k, _):
        cols = pl.ds(pl.multiple_of(k * feat, feat), feat)
        branches[k] = jnp.dot(att16[...], wo[:, cols], preferred_element_type=F32).astype(BF16)
        return 0

    lax.fori_loop(0, n_mp, branch_chunk, 0)


def scatter_kernel(
    n_dp, n_mp,
    enc_terms, branches, tok, gain_post, enc, gain_enc, inverse, asker,
    mixed_out, ffn_out, denc_out,
    e_near, e_pair, e_far, b_near, b_pair, b_far, d_norm, back_out, back_in, sq_mine, sq_all,
    near_send, near_recv, far_send, far_recv, row_send, row_recv, sq_send, sq_recv,
):
    d, m, n_x, x, c, partner = place(n_dp, n_mp)
    own_rows = enc.shape[0]
    seq_len, feat = tok.shape
    greet(n_dp, n_mp, d, m)

    def near(buf, land, t, i):
        return pltpu.make_async_remote_copy(
            src_ref=buf.at[i * 2 + 1 - c], dst_ref=land.at[i],
            send_sem=near_send.at[t, i], recv_sem=near_recv.at[t, i],
            device_id=(d, partner), device_id_type=MESH,
        )

    def far(buf, land, t, o):
        to = (x + o) % n_x
        return pltpu.make_async_remote_copy(
            src_ref=buf.at[to], dst_ref=land.at[o],
            send_sem=far_send.at[t, o], recv_sem=far_recv.at[t, o],
            device_id=(d, to * 2 + c), device_id_type=MESH,
        )

    def row_copy(s, src, dst):
        return pltpu.make_async_remote_copy(
            src_ref=back_out.at[src], dst_ref=back_in.at[dst],
            send_sem=row_send.at[s], recv_sem=row_recv.at[s],
            device_id=((d + s) % n_dp, m), device_id_type=MESH,
        )

    def sq_copy(s):
        return pltpu.make_async_remote_copy(
            src_ref=sq_mine, dst_ref=sq_all.at[s], send_sem=sq_send.at[s], recv_sem=sq_recv.at[s],
            device_id=(d, (m + s) % n_mp), device_id_type=MESH,
        )

    sets = ((enc_terms, e_near, e_pair, e_far), (branches, b_near, b_pair, b_far))
    for t, (buf, land, _, _) in enumerate(sets):
        for i in range(n_x):
            near(buf, land, t, i).start()
    for t, (buf, land, pair, beyond) in enumerate(sets):
        for i in range(n_x):
            near(buf, land, t, i).wait_recv()
        for i in range(n_x):
            pair[i] = (buf[i * 2 + c].astype(F32) + land[i].astype(F32)).astype(BF16)
        for o in range(1, n_x):
            far(pair, beyond, t, o).start()
    total = e_pair[x].astype(F32)
    for o in range(1, n_x):
        far(e_pair, e_far, 0, o).wait_recv()
        total = total + e_far[o].astype(F32)
    d_norm[...] = total.astype(BF16)
    back_in[d] = d_norm[inverse[d]]
    for s in range(1, n_dp):
        holder = (d + s) % n_dp
        back_out[holder] = d_norm[inverse[holder]]
        row_copy(s, holder, d).start()
    added = b_pair[x].astype(F32)
    for o in range(1, n_x):
        far(b_pair, b_far, 1, o).wait_recv()
        added = added + b_far[o].astype(F32)
    mixed = (tok[...].astype(F32) + added).astype(BF16)
    mixed_out[...] = mixed
    wide = mixed.astype(F32)
    squares = jnp.broadcast_to(jnp.sum(wide * wide, axis=-1, keepdims=True), (seq_len, 128))
    sq_mine[...] = jnp.transpose(squares)[:8]
    for s in range(1, n_mp):
        sq_copy(s).start()
    for s in range(1, n_dp):
        source = (d + n_dp - s) % n_dp
        row_copy(s, source, source).wait_recv()
    for row in range(own_rows):
        wide = enc[row].astype(F32)
        scale = rms_scale(wide)
        hat = wide * scale
        up = gain_enc[...] * back_in[asker[row]].astype(F32)
        inner = jnp.mean(up * hat, axis=-1, keepdims=True)
        denc_out[row] = (scale * (up - hat * inner)).astype(BF16)
    squares = sq_mine[...]
    for s in range(1, n_mp):
        sq_copy(s).wait_recv()
        squares = squares + sq_all[s]
    squares = jnp.transpose(jnp.broadcast_to(squares[:1], (128, seq_len)))[:, :1]
    scale = lax.rsqrt(squares / (feat * n_mp) + EPS)
    ffn_out[...] = (mixed_out[...].astype(F32) * scale * gain_post[m]).astype(BF16)
    for t, (buf, land, pair, beyond) in enumerate(sets):
        for i in range(n_x):
            near(buf, land, t, i).wait_send()
        for o in range(1, n_x):
            far(pair, beyond, t, o).wait_send()
    for s in range(1, n_dp):
        row_copy(s, (d + s) % n_dp, d).wait_send()
    for s in range(1, n_mp):
        sq_copy(s).wait_send()


def shards(
    tokens, cotangent, gain_dec, w_query, w_out, encodings, gain_enc, w_key, w_value, gain_post,
    neighbour_ids,
):
    n_dp, n_mp = lax.axis_size("dp"), lax.axis_size("mp")
    n_x = n_mp // 2
    seq_len, feat = tokens.shape
    head_cols = w_query.shape[1]
    own_rows, share, width = encodings.shape
    readings = neighbour_ids.shape[0] * neighbour_ids.shape[1]
    chosen = neighbour_ids.reshape(readings)
    owner = chosen // own_rows
    ids = jnp.broadcast_to(chosen[:, None], (readings, 128))
    vmem = pl.BlockSpec(memory_space=pltpu.VMEM)
    smem = pl.BlockSpec(memory_space=pltpu.SMEM)
    anywhere = pl.BlockSpec(memory_space=pl.ANY)
    dma = pltpu.SemaphoreType.DMA
    shape = jax.ShapeDtypeStruct
    limit = 58 * 1024 * 1024
    gain_enc = gain_enc.reshape(1, width)
    queries, d_att, keys, values, idtab = pl.pallas_call(
        functools.partial(gather_kernel, n_dp, n_mp),
        out_shape=(
            shape((seq_len, head_cols), BF16),
            shape((seq_len, head_cols), BF16),
            shape((readings, NLEN, head_cols), BF16),
            shape((readings, NLEN, head_cols), BF16),
            shape((n_dp, readings, 128), jnp.int32),
        ),
        in_specs=[vmem, vmem, vmem, anywhere, anywhere, vmem, vmem, anywhere, anywhere, vmem, smem],
        out_specs=(vmem,) * 5,
        scratch_shapes=[
            pltpu.VMEM((n_mp, seq_len, feat), BF16),
            pltpu.VMEM((n_mp, seq_len, feat), BF16),
            pltpu.VMEM((n_mp, readings, share, width), BF16),
            pltpu.VMEM((n_mp, seq_len, feat), BF16),
            pltpu.VMEM((n_mp, feat, head_cols), BF16),
            pltpu.VMEM(w_out.shape, BF16),
            pltpu.VMEM(w_key.shape, BF16),
            pltpu.VMEM(w_value.shape, BF16),
            pltpu.VMEM((own_rows, share, width), F32),
            pltpu.VMEM((n_dp, share, width), BF16),
            pltpu.VMEM((n_dp, share, width), BF16),
            dma((4,)),
            dma((3, 2 * n_x)),
            dma((3, 2 * n_x)),
            dma((n_dp,)),
            dma((n_dp,)),
            dma((n_dp,)),
            dma((n_dp,)),
        ],
        compiler_params=pltpu.CompilerParams(
            collective_id=0, has_side_effects=True, vmem_limit_bytes=limit
        ),
        name="gather_project",
    )(
        tokens, cotangent, gain_dec.reshape(n_mp, 1, feat), w_query.reshape(n_mp, feat, head_cols),
        w_out, encodings, gain_enc, w_key, w_value, ids, owner,
    )
    enc_terms, branches = pl.pallas_call(
        functools.partial(attend_kernel, n_mp),
        out_shape=(
            shape((n_mp, readings, share, width), BF16),
            shape((n_mp, seq_len, feat), BF16),
        ),
        in_specs=[vmem] * 4 + [anywhere] * 3,
        out_specs=(vmem, vmem),
        scratch_shapes=[
            pltpu.VMEM((readings, NLEN, head_cols), BF16),
            pltpu.VMEM((readings, NLEN, head_cols), BF16),
            pltpu.VMEM((seq_len, head_cols), F32),
            pltpu.VMEM((seq_len, head_cols), BF16),
            pltpu.VMEM(w_key.shape, BF16),
            pltpu.VMEM(w_value.shape, BF16),
            pltpu.VMEM(w_out.shape, BF16),
            dma((3,)),
        ],
        compiler_params=pltpu.CompilerParams(vmem_limit_bytes=limit),
        name="attend",
    )(queries, d_att, keys, values, w_key, w_value, w_out)
    places = jnp.arange(n_dp, dtype=jnp.int32)
    order = jnp.arange(readings, dtype=jnp.int32)
    inverse = jnp.sum(
        jnp.where(owner[None, :] == places[:, None], order[None, :], 0), axis=1, dtype=jnp.int32
    )
    held = lax.axis_index("dp") * own_rows + jnp.arange(own_rows, dtype=jnp.int32)
    asks = jnp.any(idtab[:, :, 0][None] == held[:, None, None], axis=2)
    asker = jnp.sum(jnp.where(asks, places[None, :], 0), axis=1, dtype=jnp.int32)
    return pl.pallas_call(
        functools.partial(scatter_kernel, n_dp, n_mp),
        out_shape=(
            shape((seq_len, feat), BF16),
            shape((seq_len, feat), BF16),
            shape((own_rows, share, width), BF16),
        ),
        in_specs=[vmem] * 6 + [smem] * 2,
        out_specs=(vmem,) * 3,
        scratch_shapes=[
            pltpu.VMEM((n_x, readings, share, width), BF16),
            pltpu.VMEM((n_x, readings, share, width), BF16),
            pltpu.VMEM((n_x, readings, share, width), BF16),
            pltpu.VMEM((n_x, seq_len, feat), BF16),
            pltpu.VMEM((n_x, seq_len, feat), BF16),
            pltpu.VMEM((n_x, seq_len, feat), BF16),
            pltpu.VMEM((readings, share, width), BF16),
            pltpu.VMEM((n_dp, share, width), BF16),
            pltpu.VMEM((n_dp, share, width), BF16),
            pltpu.VMEM((8, seq_len), F32),
            pltpu.VMEM((n_mp, 8, seq_len), F32),
            dma((2, n_x)),
            dma((2, n_x)),
            dma((2, n_x)),
            dma((2, n_x)),
            dma((n_dp,)),
            dma((n_dp,)),
            dma((n_mp,)),
            dma((n_mp,)),
        ],
        compiler_params=pltpu.CompilerParams(
            collective_id=1, has_side_effects=True, vmem_limit_bytes=limit
        ),
        name="reduce_return",
    )(
        enc_terms, branches, tokens, gain_post.reshape(n_mp, 1, feat), encodings, gain_enc,
        inverse, asker,
    )


def solution(mesh):
    in_specs = (
        P("dp", "mp"),
        P("dp", "mp"),
        P(),
        P(None, "mp"),
        P("mp", None),
        P("dp", "mp", None),
        P(),
        P(None, "mp"),
        P(None, "mp"),
        P(),
        P("dp", None),
    )
    out_specs = (P("dp", "mp"), P("dp", "mp"), P("dp", "mp", None))
    return jax.shard_map(shards, mesh=mesh, in_specs=in_specs, out_specs=out_specs, check_vma=False)
```

```python
import functools

import jax
import jax.numpy as jnp
from jax import lax
from jax.experimental import pallas as pl
from jax.experimental.pallas import tpu as pltpu
from jax.sharding import PartitionSpec as P

HD = 128
BLOCK = 64
NLEN = 128
NEIGH = 2
LEAD = BLOCK - 1
EPS = 1e-06
MESH = pl.DeviceIdType.MESH
BF16 = jnp.bfloat16
F32 = jnp.float32
NT = (((1,), (1,)), ((), ()))
TN = (((0,), (0,)), ((), ()))


def rms_scale(values):
    return lax.rsqrt(jnp.mean(values * values, axis=-1, keepdims=True) + EPS)


def place(n_dp, n_mp):
    d, m = lax.axis_index("dp"), lax.axis_index("mp")
    n_x = n_mp // 2
    x, c = m // 2, m % 2
    return d, m, n_x, x, c, x * 2 + (1 - c)


def greet(n_dp, n_mp, d, m):
    barrier = pltpu.get_barrier_semaphore()
    for s in range(1, n_dp):
        pl.semaphore_signal(barrier, inc=1, device_id=((d + s) % n_dp, m), device_id_type=MESH)
    for s in range(1, n_mp):
        pl.semaphore_signal(barrier, inc=1, device_id=(d, (m + s) % n_mp), device_id_type=MESH)
    pl.semaphore_wait(barrier, n_dp + n_mp - 2)


def layer_kernel(
    n_dp, n_mp,
    tok, cot, gain_dec, wq_hbm, wo_hbm, enc, gain_enc, wk_hbm, wv_hbm, chosen,
    mixed_out, squares_out, rows_out,
    tok_all, cot_a, cot_b, enc_all, normed, wq, wo, wk, wv, enc_norm, sending, arrived, ids, idtab,
    q, da, keys, values, prob_all, att, att16, dk, dv,
    enc_terms, branches, e_near, e_pair, e_far, b_near, b_pair, b_far,
    d_norm, back_out, back_in, sq_mine, sq_all,
    w_sem, ag_send, ag_recv, id_send, id_recv, row_send, row_recv,
    near_send, near_recv, far_send, far_recv, back_send, back_recv, sq_send, sq_recv,
):
    d, m, n_x, x, c, partner = place(n_dp, n_mp)
    own_rows, share, width = enc.shape
    readings = ids.shape[0]
    seq_len, feat = tok.shape
    half = seq_len // 2
    head_cols = wq.shape[2]
    heads = head_cols // HD
    factor = HD ** (-0.5)
    loads = [
        pltpu.make_async_copy(a, b, w_sem.at[i])
        for i, (a, b) in enumerate([(wq_hbm, wq), (wo_hbm, wo), (wk_hbm, wk), (wv_hbm, wv)])
    ]
    for i in (0, 2, 3, 1):
        loads[i].start()

    def hop(buf, t, kind, chunk, target):
        return pltpu.make_async_remote_copy(
            src_ref=buf.at[chunk], dst_ref=buf.at[chunk],
            send_sem=ag_send.at[t, kind], recv_sem=ag_recv.at[t, kind],
            device_id=(d, target), device_id_type=MESH,
        )

    def spread(buf, t):
        for o in range(1, n_x):
            hop(buf, t, o, m, ((x + o) % n_x) * 2 + c).start()
        hop(buf, t, 0, m, partner).start()

    def forward(buf, t):
        for o in range(1, n_x):
            chunk = ((x + n_x - o) % n_x) * 2 + c
            hop(buf, t, o, chunk, partner).wait_recv()
            hop(buf, t, n_x + o, chunk, partner).start()

    def finish(buf, t):
        hop(buf, t, 0, partner, partner).wait_recv()
        for o in range(1, n_x):
            hop(buf, t, n_x + o, ((x + n_x - o) % n_x) * 2 + 1 - c, partner).wait_recv()

    def sent_far(buf, t):
        for o in range(1, n_x):
            hop(buf, t, o, m, partner).wait_send()

    def sent_near(buf, t):
        hop(buf, t, 0, m, partner).wait_send()
        for o in range(1, n_x):
            hop(buf, t, n_x + o, m, partner).wait_send()

    def dp_copy(src, dst, send, recv, s):
        return pltpu.make_async_remote_copy(
            src_ref=src, dst_ref=dst, send_sem=send.at[s], recv_sem=recv.at[s],
            device_id=((d + s) % n_dp, m), device_id_type=MESH,
        )

    def id_copy(s, to):
        return dp_copy(ids, idtab.at[to], id_send, id_recv, s)

    def row_copy(s, src, dst):
        return dp_copy(sending.at[src], arrived.at[dst], row_send, row_recv, s)

    def back_copy(s, src, dst):
        return dp_copy(back_out.at[src], back_in.at[dst], back_send, back_recv, s)

    def near(buf, land, t, i):
        return pltpu.make_async_remote_copy(
            src_ref=buf.at[i * 2 + 1 - c], dst_ref=land.at[i],
            send_sem=near_send.at[t, i], recv_sem=near_recv.at[t, i],
            device_id=(d, partner), device_id_type=MESH,
        )

    def far(buf, land, t, o):
        to = (x + o) % n_x
        return pltpu.make_async_remote_copy(
            src_ref=buf.at[to], dst_ref=land.at[o],
            send_sem=far_send.at[t, o], recv_sem=far_recv.at[t, o],
            device_id=(d, to * 2 + c), device_id_type=MESH,
        )

    def sq_copy(s):
        return pltpu.make_async_remote_copy(
            src_ref=sq_mine, dst_ref=sq_all.at[s], send_sem=sq_send.at[s], recv_sem=sq_recv.at[s],
            device_id=(d, (m + s) % n_mp), device_id_type=MESH,
        )

    def pair_up(buf, land, pair, t):
        for i in range(n_x):
            near(buf, land, t, i).wait_recv()
        for o in range(1, n_x):
            to = (x + o) % n_x
            pair[to] = (buf[to * 2 + c].astype(F32) + land[to].astype(F32)).astype(BF16)

    tok_all[m] = tok[...]
    picks = [chosen[a // NEIGH, a % NEIGH] for a in range(readings)]
    spot = lax.broadcasted_iota(jnp.int32, (readings, 128), 0)
    listed = jnp.zeros((readings, 128), jnp.int32)
    for a in range(readings):
        listed = jnp.where(spot == a, picks[a], listed)
    ids[...] = listed
    greet(n_dp, n_mp, d, m)
    for s in range(1, n_dp):
        id_copy(s, d).start()
    spread(tok_all, 0)
    idtab[d] = listed
    cot_a[m] = cot[:half]
    cot_b[m] = cot[half:]
    wide = enc[...].astype(F32)
    enc_norm[...] = wide * rms_scale(wide) * gain_enc[...][None]

    def choose(reader):
        asked = idtab[reader]
        total = jnp.zeros((share, width), F32)
        for row in range(own_rows):
            hit = jnp.where(asked == d * own_rows + row, 1.0, 0.0).astype(F32)
            hit = jnp.max(hit, axis=0, keepdims=True)
            total = total + enc_norm[row] * jnp.concatenate([hit] * (width // 128), axis=1)
        return total.astype(BF16)

    for s in range(1, n_dp):
        reader = (d + s) % n_dp
        id_copy(n_dp - s, reader).wait_recv()
        sending[reader] = choose(reader)
        row_copy(s, reader, d).start()
    arrived[d] = choose(d)
    sent_far(tok_all, 0)
    spread(cot_a, 1)
    forward(tok_all, 0)
    table = idtab[...]
    owner_at = lax.broadcasted_iota(jnp.int32, table.shape, 0)
    askers = [
        jnp.max(jnp.where(table == d * own_rows + row, owner_at, 0)) for row in range(own_rows)
    ]
    for s in range(1, n_dp):
        holder = (d + n_dp - s) % n_dp
        row_copy(s, holder, holder).wait_recv()
    for a in range(readings):
        enc_all[m, a] = arrived[picks[a] // own_rows]
    spread(enc_all, 3)
    finish(tok_all, 0)
    squares = jnp.zeros((seq_len, 1), F32)
    for k in range(n_mp):
        part = tok_all[k].astype(F32)
        squares = squares + jnp.sum(part * part, axis=-1, keepdims=True)
    scale = lax.rsqrt(squares / (feat * n_mp) + EPS)
    for k in range(n_mp):
        normed[k] = (tok_all[k].astype(F32) * scale * gain_dec[k]).astype(BF16)
    loads[0].wait()
    keep = lax.broadcasted_iota(jnp.int32, (seq_len, 256), 0) < seq_len - LEAD

    def shift_up(part):
        return jnp.where(keep, pltpu.roll(part, seq_len - LEAD, 0), 0.0).astype(BF16)

    def query_tile(n, _):
        cols = pl.ds(pl.multiple_of(n * 256, 256), 256)
        acc = jnp.zeros((seq_len, 256), F32)
        for k in range(n_mp):
            acc += jnp.dot(normed[k], wq[k, :, cols], preferred_element_type=F32)
        q[:, cols] = shift_up(acc)
        return 0

    lax.fori_loop(0, head_cols // 256, query_tile, 0)
    forward(cot_a, 1)
    sent_far(enc_all, 3)
    spread(cot_b, 2)
    forward(enc_all, 3)
    finish(enc_all, 3)
    loads[2].wait()
    loads[3].wait()

    def memory_tile(n, _):
        cols = pl.ds(pl.multiple_of(n * 256, 256), 256)
        for k in range(n_mp):
            rows = enc_all[k].reshape(readings * share, width)
            for weight, out in ((wk, keys), (wv, values)):
                part = jnp.dot(rows, weight[:, cols], preferred_element_type=F32).astype(BF16)
                out[:, k * share : (k + 1) * share, cols] = part.reshape(readings, share, 256)
        return 0

    lax.fori_loop(0, head_cols // 256, memory_tile, 0)

    def memory_of(buf, b, h):
        part = buf[pl.ds(b * NEIGH, NEIGH), :, h * HD : (h + 1) * HD]
        return part.reshape(NEIGH * NLEN, HD)

    def attend(b, _):
        rows = pl.ds(pl.multiple_of(b * BLOCK, BLOCK), BLOCK)
        for h0 in range(0, heads, 4):
            group = range(h0, h0 + 4)
            scores = [
                lax.dot_general(
                    q[rows, h * HD : (h + 1) * HD], memory_of(keys, b, h), NT,
                    preferred_element_type=F32,
                ) * factor
                for h in group
            ]
            lifted = [jnp.exp(v - jnp.max(v, axis=-1, keepdims=True)) for v in scores]
            prob = [v / jnp.sum(v, axis=-1, keepdims=True) for v in lifted]
            for h, v in zip(group, prob):
                prob_all[b, h] = v
            for h, v in zip(group, prob):
                att[rows, h * HD : (h + 1) * HD] = jnp.dot(
                    v.astype(BF16), memory_of(values, b, h), preferred_element_type=F32
                )
        return 0

    lax.fori_loop(0, seq_len // BLOCK, attend, 0)
    low = lax.broadcasted_iota(jnp.int32, (seq_len, head_cols), 0) >= LEAD
    att16[...] = jnp.where(low, pltpu.roll(att[...], LEAD, 0), 0.0).astype(BF16)
    loads[1].wait()

    def branch_chunk(k, _):
        cols = pl.ds(pl.multiple_of(k * feat, feat), feat)
        branches[k] = jnp.dot(att16[...], wo[:, cols], preferred_element_type=F32).astype(BF16)
        return 0

    lax.fori_loop(0, n_mp, branch_chunk, 0)
    for i in range(n_x):
        near(branches, b_near, 1, i).start()
    forward(cot_b, 2)
    pair_up(branches, b_near, b_pair, 1)
    for o in range(1, n_x):
        far(b_pair, b_far, 1, o).start()
    finish(cot_a, 1)
    finish(cot_b, 2)

    def grad_tile(n, _):
        cols = pl.ds(pl.multiple_of(n * 256, 256), 256)
        acc = jnp.zeros((seq_len, 256), F32)
        for k in range(n_mp):
            acc += lax.dot_general(
                jnp.concatenate([cot_a[k], cot_b[k]], axis=0),
                wo[cols, k * feat : (k + 1) * feat], NT, preferred_element_type=F32,
            )
        da[:, cols] = shift_up(acc)
        return 0

    lax.fori_loop(0, head_cols // 256, grad_tile, 0)

    def attend_back(b, _):
        rows = pl.ds(pl.multiple_of(b * BLOCK, BLOCK), BLOCK)
        mem = pl.ds(b * NEIGH, NEIGH)
        for h0 in range(0, heads, 4):
            group = range(h0, h0 + 4)
            d_prob = [
                lax.dot_general(
                    da[rows, h * HD : (h + 1) * HD], memory_of(values, b, h), NT,
                    preferred_element_type=F32,
                )
                for h in group
            ]
            for h in group:
                cols = slice(h * HD, (h + 1) * HD)
                dv_h = lax.dot_general(
                    prob_all[b, h].astype(BF16), da[rows, cols], TN, preferred_element_type=F32
                )
                dv[mem, :, cols] = dv_h.astype(BF16).reshape(NEIGH, NLEN, HD)
            d_scores = []
            for h, v in zip(group, d_prob):
                prob = prob_all[b, h]
                inner = jnp.sum(prob * v, axis=-1, keepdims=True)
                d_scores.append((prob * (v - inner) * factor).astype(BF16))
            for h, v in zip(group, d_scores):
                cols = slice(h * HD, (h + 1) * HD)
                dk_h = lax.dot_general(v, q[rows, cols], TN, preferred_element_type=F32)
                dk[mem, :, cols] = dk_h.astype(BF16).reshape(NEIGH, NLEN, HD)
        return 0

    lax.fori_loop(0, seq_len // BLOCK, attend_back, 0)

    def enc_chunk(k):
        toks = pl.ds(pl.multiple_of(k * share, share), share)
        acc = lax.dot_general(
            dk[:, toks, :].reshape(readings * share, head_cols), wk[...], NT,
            preferred_element_type=F32,
        )
        acc += lax.dot_general(
            dv[:, toks, :].reshape(readings * share, head_cols), wv[...], NT,
            preferred_element_type=F32,
        )
        enc_terms[k] = acc.astype(BF16).reshape(readings, share, width)

    def partner_chunk(i, _):
        enc_chunk(i * 2 + 1 - c)
        near(enc_terms, e_near, 0, i).start()
        return 0

    def own_chunk(i, _):
        enc_chunk(i * 2 + c)
        return 0

    lax.fori_loop(0, n_x, partner_chunk, 0)
    lax.fori_loop(0, n_x, own_chunk, 0)
    pair_up(enc_terms, e_near, e_pair, 0)
    for o in range(1, n_x):
        far(e_pair, e_far, 0, o).start()
    added = branches[m].astype(F32) + b_near[x].astype(F32)
    for o in range(1, n_x):
        far(b_pair, b_far, 1, o).wait_recv()
        added = added + b_far[o].astype(F32)
    mixed = (tok[...].astype(F32) + added).astype(BF16)
    mixed_out[...] = mixed
    wide = mixed.astype(F32)
    squares = jnp.broadcast_to(jnp.sum(wide * wide, axis=-1, keepdims=True), (seq_len, 128))
    sq_mine[...] = jnp.transpose(squares)[:8]
    for s in range(1, n_mp):
        sq_copy(s).start()
    total = enc_terms[m].astype(F32) + e_near[x].astype(F32)
    for o in range(1, n_x):
        far(e_pair, e_far, 0, o).wait_recv()
        total = total + e_far[o].astype(F32)
    d_norm[...] = total.astype(BF16)

    def reading_of(holder):
        found = jnp.int32(0)
        for a in range(readings):
            found = jnp.where(picks[a] // own_rows == holder, a, found)
        return found

    for s in range(1, n_dp):
        holder = (d + s) % n_dp
        back_out[holder] = d_norm[reading_of(holder)]
        back_copy(s, holder, d).start()
    back_in[d] = d_norm[reading_of(d)]
    squares = sq_mine[...]
    for s in range(1, n_mp):
        sq_copy(s).wait_recv()
        squares = squares + sq_all[s]
    squares_out[...] = squares
    for s in range(1, n_dp):
        source = (d + n_dp - s) % n_dp
        back_copy(s, source, source).wait_recv()
    for row in range(own_rows):
        rows_out[row] = back_in[askers[row]]
    sent_far(cot_a, 1)
    sent_far(cot_b, 2)
    for t, buf in enumerate((tok_all, cot_a, cot_b, enc_all)):
        sent_near(buf, t)
    for t, (buf, land, pair, beyond) in enumerate(
        ((enc_terms, e_near, e_pair, e_far), (branches, b_near, b_pair, b_far))
    ):
        for i in range(n_x):
            near(buf, land, t, i).wait_send()
        for o in range(1, n_x):
            far(pair, beyond, t, o).wait_send()
    for s in range(1, n_dp):
        to = (d + s) % n_dp
        id_copy(s, d).wait_send()
        row_copy(s, to, d).wait_send()
        back_copy(s, to, d).wait_send()
    for s in range(1, n_mp):
        sq_copy(s).wait_send()


def finish_kernel(n_mp, mixed, squares, rows, enc, gain_enc, gain_post, mixed_out, ffn_out, denc_out):
    seq_len, feat = mixed.shape
    mixed_out[...] = mixed[...]
    scale = jnp.transpose(jnp.broadcast_to(squares[:1], (128, seq_len)))[:, :1]
    scale = lax.rsqrt(scale / (feat * n_mp) + EPS)
    gain = gain_post[lax.axis_index("mp")]
    ffn_out[...] = (mixed[...].astype(F32) * scale * gain).astype(BF16)
    for row in range(enc.shape[0]):
        wide = enc[row].astype(F32)
        scale = rms_scale(wide)
        hat = wide * scale
        up = gain_enc[...] * rows[row].astype(F32)
        inner = jnp.mean(up * hat, axis=-1, keepdims=True)
        denc_out[row] = (scale * (up - hat * inner)).astype(BF16)


def shards(
    tokens, cotangent, gain_dec, w_query, w_out, encodings, gain_enc, w_key, w_value, gain_post,
    neighbour_ids,
):
    n_dp, n_mp = lax.axis_size("dp"), lax.axis_size("mp")
    n_x = n_mp // 2
    seq_len, feat = tokens.shape
    head_cols = w_query.shape[1]
    own_rows, share, width = encodings.shape
    blocks = neighbour_ids.shape[0]
    readings = blocks * neighbour_ids.shape[1]
    block = pl.BlockSpec(memory_space=pltpu.VMEM)
    smem = pl.BlockSpec(memory_space=pltpu.SMEM)
    anywhere = pl.BlockSpec(memory_space=pl.ANY)
    dma = pltpu.SemaphoreType.DMA
    shape = jax.ShapeDtypeStruct
    vmem = pltpu.VMEM
    gain_enc = gain_enc.reshape(1, width)
    tokens_all = vmem((n_mp, seq_len, feat), BF16)
    half_all = vmem((n_mp, seq_len // 2, feat), BF16)
    rows_all = vmem((n_mp, readings, share, width), BF16)
    slots = vmem((n_dp, share, width), BF16)
    local = vmem((seq_len, head_cols), BF16)
    memory = vmem((readings, NLEN, head_cols), BF16)
    rows_x = vmem((n_x, readings, share, width), BF16)
    tokens_x = vmem((n_x, seq_len, feat), BF16)
    mixed, squares, rows = pl.pallas_call(
        functools.partial(layer_kernel, n_dp, n_mp),
        out_shape=(
            shape((seq_len, feat), BF16),
            shape((8, seq_len), F32),
            shape((own_rows, share, width), BF16),
        ),
        in_specs=[block] * 3 + [anywhere] * 2 + [block] * 2 + [anywhere] * 2 + [smem],
        out_specs=(block,) * 3,
        scratch_shapes=[
            tokens_all, half_all, half_all, rows_all, tokens_all,
            vmem((n_mp, feat, head_cols), BF16),
            vmem(w_out.shape, BF16),
            vmem(w_key.shape, BF16),
            vmem(w_value.shape, BF16),
            vmem((own_rows, share, width), F32),
            slots, slots,
            vmem((readings, 128), jnp.int32),
            vmem((n_dp, readings, 128), jnp.int32),
            local, local, memory, memory,
            vmem((blocks, head_cols // HD, BLOCK, NEIGH * NLEN), F32),
            vmem((seq_len, head_cols), F32),
            local, memory, memory,
            rows_all, tokens_all,
            rows_x, rows_x, rows_x, tokens_x, tokens_x, tokens_x,
            vmem((readings, share, width), BF16),
            slots, slots,
            vmem((8, seq_len), F32),
            vmem((n_mp, 8, seq_len), F32),
            dma((4,)),
            dma((4, 2 * n_x)), dma((4, 2 * n_x)),
            dma((n_dp,)), dma((n_dp,)), dma((n_dp,)), dma((n_dp,)),
            dma((2, n_x)), dma((2, n_x)), dma((2, n_x)), dma((2, n_x)),
            dma((n_dp,)), dma((n_dp,)), dma((n_mp,)), dma((n_mp,)),
        ],
        compiler_params=pltpu.CompilerParams(
            collective_id=0, has_side_effects=True, vmem_limit_bytes=60 * 1024 * 1024
        ),
        name="layer",
    )(
        tokens, cotangent, gain_dec.reshape(n_mp, 1, feat), w_query.reshape(n_mp, feat, head_cols),
        w_out, encodings, gain_enc, w_key, w_value, neighbour_ids,
    )
    return pl.pallas_call(
        functools.partial(finish_kernel, n_mp),
        out_shape=(
            shape((seq_len, feat), BF16),
            shape((seq_len, feat), BF16),
            shape((own_rows, share, width), BF16),
        ),
        in_specs=[block] * 6,
        out_specs=(block,) * 3,
        name="finish",
    )(mixed, squares, rows, encodings, gain_enc, gain_post.reshape(n_mp, 1, feat))


def solution(mesh):
    in_specs = (
        P("dp", "mp"),
        P("dp", "mp"),
        P(),
        P(None, "mp"),
        P("mp", None),
        P("dp", "mp", None),
        P(),
        P(None, "mp"),
        P(None, "mp"),
        P(),
        P("dp", None),
    )
    out_specs = (P("dp", "mp"), P("dp", "mp"), P("dp", "mp", None))
    return jax.shard_map(shards, mesh=mesh, in_specs=in_specs, out_specs=out_specs, check_vma=False)
```

```python
import functools

import jax
import jax.numpy as jnp
from jax import lax
from jax.experimental import pallas as pl
from jax.experimental.pallas import tpu as pltpu
from jax.sharding import PartitionSpec as P

HD = 128
BLOCK = 64
NLEN = 128
NEIGH = 2
LEAD = BLOCK - 1
EPS = 1e-06
MESH = pl.DeviceIdType.MESH
BF16 = jnp.bfloat16
F32 = jnp.float32
NT = (((1,), (1,)), ((), ()))
TN = (((0,), (0,)), ((), ()))


def rms_scale(values):
    return lax.rsqrt(jnp.mean(values * values, axis=-1, keepdims=True) + EPS)


def row_of(gain):
    return jnp.concatenate([gain[i : i + 1] for i in range(gain.shape[0])], axis=1)


def place(n_dp, n_mp):
    d, m = lax.axis_index("dp"), lax.axis_index("mp")
    n_x = n_mp // 2
    x, c = m // 2, m % 2
    return d, m, n_x, x, c, x * 2 + (1 - c)


def greet(n_dp, n_mp, d, m):
    barrier = pltpu.get_barrier_semaphore()
    for s in range(1, n_dp):
        pl.semaphore_signal(barrier, inc=1, device_id=((d + s) % n_dp, m), device_id_type=MESH)
    for s in range(1, n_mp):
        pl.semaphore_signal(barrier, inc=1, device_id=(d, (m + s) % n_mp), device_id_type=MESH)
    pl.semaphore_wait(barrier, n_dp + n_mp - 2)


def layer_kernel(
    n_dp, n_mp,
    tok, cot, gain_dec, wq_hbm, wo_hbm, enc, gain_enc, wk_hbm, wv_hbm, chosen,
    mixed_out, squares_out, rows_out,
    tok_all, cot_a, cot_b, enc_all, normed, wq, wo, wk, wv, enc_norm, sending, arrived, ids, idtab,
    q, da, keys, values, prob_all, att, att16, dk, dv,
    enc_terms, branches, e_near, e_pair, e_far, b_near, b_pair, b_far,
    d_norm, back_out, back_in, sq_mine, sq_all,
    w_sem, ag_send, ag_recv, id_send, id_recv, row_send, row_recv,
    near_send, near_recv, far_send, far_recv, back_send, back_recv, sq_send, sq_recv,
):
    d, m, n_x, x, c, partner = place(n_dp, n_mp)
    own_rows, share, width = enc.shape
    readings = ids.shape[0]
    seq_len, feat = tok.shape
    half = seq_len // 2
    head_cols = wq.shape[2]
    heads = head_cols // HD
    factor = HD ** (-0.5)
    cut = width // 256 * 128
    spans = (slice(0, cut), slice(cut, width), slice(0, feat))
    loads = [
        pltpu.make_async_copy(a, b, w_sem.at[i])
        for i, (a, b) in enumerate([(wq_hbm, wq), (wo_hbm, wo), (wk_hbm, wk), (wv_hbm, wv)])
    ]
    for i in (0, 2, 3, 1):
        loads[i].start()

    def hop(buf, t, kind, chunk, target):
        return pltpu.make_async_remote_copy(
            src_ref=buf.at[chunk], dst_ref=buf.at[chunk],
            send_sem=ag_send.at[t, kind], recv_sem=ag_recv.at[t, kind],
            device_id=(d, target), device_id_type=MESH,
        )

    def spread(buf, t):
        for o in range(1, n_x):
            hop(buf, t, o, m, ((x + o) % n_x) * 2 + c).start()
        hop(buf, t, 0, m, partner).start()

    def forward(buf, t):
        for o in range(1, n_x):
            chunk = ((x + n_x - o) % n_x) * 2 + c
            hop(buf, t, o, chunk, partner).wait_recv()
            hop(buf, t, n_x + o, chunk, partner).start()

    def finish(buf, t):
        hop(buf, t, 0, partner, partner).wait_recv()
        for o in range(1, n_x):
            hop(buf, t, n_x + o, ((x + n_x - o) % n_x) * 2 + 1 - c, partner).wait_recv()

    def sent_far(buf, t):
        for o in range(1, n_x):
            hop(buf, t, o, m, partner).wait_send()

    def sent_near(buf, t):
        hop(buf, t, 0, m, partner).wait_send()
        for o in range(1, n_x):
            hop(buf, t, n_x + o, m, partner).wait_send()

    def dp_copy(src, dst, send, recv, s):
        return pltpu.make_async_remote_copy(
            src_ref=src, dst_ref=dst, send_sem=send.at[s], recv_sem=recv.at[s],
            device_id=((d + s) % n_dp, m), device_id_type=MESH,
        )

    def id_copy(s, to):
        return dp_copy(ids, idtab.at[to], id_send, id_recv, s)

    def row_copy(s, src, dst):
        return dp_copy(sending.at[src], arrived.at[dst], row_send, row_recv, s)

    def back_copy(t, s, src, dst):
        cols = spans[t]
        return dp_copy(
            back_out.at[src, :, cols], back_in.at[dst, :, cols],
            back_send.at[t], back_recv.at[t], s,
        )

    def near(buf, land, t, i):
        cols = spans[t]
        return pltpu.make_async_remote_copy(
            src_ref=buf.at[i * 2 + 1 - c, ..., cols], dst_ref=land.at[i, ..., cols],
            send_sem=near_send.at[t, i], recv_sem=near_recv.at[t, i],
            device_id=(d, partner), device_id_type=MESH,
        )

    def far(buf, land, t, o):
        to, cols = (x + o) % n_x, spans[t]
        return pltpu.make_async_remote_copy(
            src_ref=buf.at[to, ..., cols], dst_ref=land.at[o, ..., cols],
            send_sem=far_send.at[t, o], recv_sem=far_recv.at[t, o],
            device_id=(d, to * 2 + c), device_id_type=MESH,
        )

    def sq_copy(s):
        return pltpu.make_async_remote_copy(
            src_ref=sq_mine, dst_ref=sq_all.at[s], send_sem=sq_send.at[s], recv_sem=sq_recv.at[s],
            device_id=(d, (m + s) % n_mp), device_id_type=MESH,
        )

    def pair_up(buf, land, pair, t):
        cols = spans[t]
        for o in range(1, n_x):
            to = (x + o) % n_x
            near(buf, land, t, to).wait_recv()
            theirs = land[to, ..., cols].astype(F32)
            pair[to, ..., cols] = (buf[to * 2 + c, ..., cols].astype(F32) + theirs).astype(BF16)

    tok_all[m] = tok[...]
    picks = [chosen[a % NEIGH, a // NEIGH] for a in range(readings)]
    spot = lax.broadcasted_iota(jnp.int32, (readings, 128), 0)
    listed = jnp.zeros((readings, 128), jnp.int32)
    for a in range(readings):
        listed = jnp.where(spot == a, picks[a], listed)
    ids[...] = listed
    greet(n_dp, n_mp, d, m)
    for s in range(1, n_dp):
        id_copy(s, d).start()
    spread(tok_all, 0)
    idtab[d] = listed
    cot_a[m] = cot[:half]
    cot_b[m] = cot[half:]
    wide = enc[...].astype(F32)
    enc_norm[...] = wide * rms_scale(wide) * row_of(gain_enc)[None]

    def choose(reader):
        asked = idtab[reader]
        total = jnp.zeros((share, width), F32)
        for row in range(own_rows):
            hit = jnp.where(asked == d * own_rows + row, 1.0, 0.0).astype(F32)
            hit = jnp.max(hit, axis=0, keepdims=True)
            total = total + enc_norm[row] * jnp.concatenate([hit] * (width // 128), axis=1)
        return total.astype(BF16)

    for s in range(1, n_dp):
        reader = (d + s) % n_dp
        id_copy(n_dp - s, reader).wait_recv()
        sending[reader] = choose(reader)
        row_copy(s, reader, d).start()
    arrived[d] = choose(d)
    sent_far(tok_all, 0)
    spread(cot_a, 1)
    forward(tok_all, 0)
    table = idtab[...]
    owner_at = lax.broadcasted_iota(jnp.int32, table.shape, 0)
    askers = [
        jnp.max(jnp.where(table == d * own_rows + row, owner_at, 0)) for row in range(own_rows)
    ]
    for s in range(1, n_dp):
        holder = (d + n_dp - s) % n_dp
        row_copy(s, holder, holder).wait_recv()
    for a in range(readings):
        enc_all[m, a] = arrived[picks[a] // own_rows]
    spread(enc_all, 3)
    finish(tok_all, 0)
    squares = jnp.zeros((seq_len, 1), F32)
    for k in range(n_mp):
        part = tok_all[k].astype(F32)
        squares = squares + jnp.sum(part * part, axis=-1, keepdims=True)
    scale = lax.rsqrt(squares / (feat * n_mp) + EPS)
    for k in range(n_mp):
        normed[k] = (tok_all[k].astype(F32) * scale * gain_dec[k]).astype(BF16)
    loads[0].wait()
    keep = lax.broadcasted_iota(jnp.int32, (seq_len, 256), 0) < seq_len - LEAD

    def shift_up(part):
        return jnp.where(keep, pltpu.roll(part, seq_len - LEAD, 0), 0.0).astype(BF16)

    def query_tile(n, _):
        cols = pl.ds(pl.multiple_of(n * 256, 256), 256)
        acc = jnp.zeros((seq_len, 256), F32)
        for k in range(n_mp):
            acc += jnp.dot(normed[k], wq[k, :, cols], preferred_element_type=F32)
        q[:, cols] = shift_up(acc)
        return 0

    lax.fori_loop(0, head_cols // 256, query_tile, 0)
    forward(cot_a, 1)
    sent_far(enc_all, 3)
    spread(cot_b, 2)
    loads[2].wait()
    loads[3].wait()

    def project_memory(k):
        toks = pl.ds(pl.multiple_of(k * share, share), share)
        rows = enc_all[k].reshape(readings * share, width)

        def tile(n, _):
            cols = pl.ds(pl.multiple_of(n * 256, 256), 256)
            for weight, out in ((wk, keys), (wv, values)):
                part = jnp.dot(rows, weight[:, cols], preferred_element_type=F32).astype(BF16)
                out[:, toks, cols] = part.reshape(readings, share, 256)
            return 0

        lax.fori_loop(0, head_cols // 256, tile, 0)

    project_memory(m)
    hop(enc_all, 3, 0, partner, partner).wait_recv()
    project_memory(partner)
    forward(enc_all, 3)
    for o in range(1, n_x):
        project_memory(((x + n_x - o) % n_x) * 2 + c)
    for o in range(1, n_x):
        chunk = ((x + n_x - o) % n_x) * 2 + 1 - c
        hop(enc_all, 3, n_x + o, chunk, partner).wait_recv()
        project_memory(chunk)

    def memory_of(buf, b, h):
        part = buf[pl.ds(b * NEIGH, NEIGH), :, h * HD : (h + 1) * HD]
        return part.reshape(NEIGH * NLEN, HD)

    def attend(b, _):
        rows = pl.ds(pl.multiple_of(b * BLOCK, BLOCK), BLOCK)
        for h0 in range(0, heads, 8):
            group = range(h0, min(h0 + 8, heads))
            scores = [
                lax.dot_general(
                    q[rows, h * HD : (h + 1) * HD], memory_of(keys, b, h), NT,
                    preferred_element_type=F32,
                ) * factor
                for h in group
            ]
            lifted = [jnp.exp(v - jnp.max(v, axis=-1, keepdims=True)) for v in scores]
            prob = [v / jnp.sum(v, axis=-1, keepdims=True) for v in lifted]
            for h, v in zip(group, prob):
                prob_all[b, h] = v
            for h, v in zip(group, prob):
                att[rows, h * HD : (h + 1) * HD] = jnp.dot(
                    v.astype(BF16), memory_of(values, b, h), preferred_element_type=F32
                )
        return 0

    lax.fori_loop(0, seq_len // BLOCK, attend, 0)
    low = lax.broadcasted_iota(jnp.int32, (seq_len, head_cols), 0) >= LEAD
    att16[...] = jnp.where(low, pltpu.roll(att[...], LEAD, 0), 0.0).astype(BF16)
    loads[1].wait()

    def branch_chunk(k, _):
        cols = pl.ds(pl.multiple_of(k * feat, feat), feat)
        branches[k] = jnp.dot(att16[...], wo[:, cols], preferred_element_type=F32).astype(BF16)
        return 0

    lax.fori_loop(0, n_mp, branch_chunk, 0)
    for i in range(n_x):
        near(branches, b_near, 2, i).start()
    forward(cot_b, 2)
    pair_up(branches, b_near, b_pair, 2)
    for o in range(1, n_x):
        far(b_pair, b_far, 2, o).start()
    finish(cot_a, 1)
    finish(cot_b, 2)

    def grad_tile(n, _):
        cols = pl.ds(pl.multiple_of(n * 256, 256), 256)
        acc = jnp.zeros((seq_len, 256), F32)
        for k in range(n_mp):
            acc += lax.dot_general(
                jnp.concatenate([cot_a[k], cot_b[k]], axis=0),
                wo[cols, k * feat : (k + 1) * feat], NT, preferred_element_type=F32,
            )
        da[:, cols] = shift_up(acc)
        return 0

    lax.fori_loop(0, head_cols // 256, grad_tile, 0)

    def attend_back(b, _):
        rows = pl.ds(pl.multiple_of(b * BLOCK, BLOCK), BLOCK)
        mem = pl.ds(b * NEIGH, NEIGH)
        for h0 in range(0, heads, 8):
            group = range(h0, min(h0 + 8, heads))
            d_prob = [
                lax.dot_general(
                    da[rows, h * HD : (h + 1) * HD], memory_of(values, b, h), NT,
                    preferred_element_type=F32,
                )
                for h in group
            ]
            for h in group:
                cols = slice(h * HD, (h + 1) * HD)
                dv_h = lax.dot_general(
                    prob_all[b, h].astype(BF16), da[rows, cols], TN, preferred_element_type=F32
                )
                dv[mem, :, cols] = dv_h.astype(BF16).reshape(NEIGH, NLEN, HD)
            d_scores = []
            for h, v in zip(group, d_prob):
                prob = prob_all[b, h]
                inner = jnp.sum(prob * v, axis=-1, keepdims=True)
                d_scores.append((prob * (v - inner) * factor).astype(BF16))
            for h, v in zip(group, d_scores):
                cols = slice(h * HD, (h + 1) * HD)
                dk_h = lax.dot_general(v, q[rows, cols], TN, preferred_element_type=F32)
                dk[mem, :, cols] = dk_h.astype(BF16).reshape(NEIGH, NLEN, HD)
        return 0

    lax.fori_loop(0, seq_len // BLOCK, attend_back, 0)

    def enc_chunk(k, t):
        toks = pl.ds(pl.multiple_of(k * share, share), share)
        cols = spans[t]
        acc = lax.dot_general(
            dk[:, toks, :].reshape(readings * share, head_cols), wk[cols, :], NT,
            preferred_element_type=F32,
        )
        acc += lax.dot_general(
            dv[:, toks, :].reshape(readings * share, head_cols), wv[cols, :], NT,
            preferred_element_type=F32,
        )
        enc_terms[k, :, :, cols] = acc.astype(BF16).reshape(readings, share, cols.stop - cols.start)

    for t in range(2):
        for o in range(1, n_x):
            to = (x + o) % n_x
            enc_chunk(to * 2 + 1 - c, t)
            near(enc_terms, e_near, t, to).start()
        for o in range(1, n_x):
            enc_chunk((x + o) % n_x * 2 + c, t)
        if t == 0:
            pair_up(enc_terms, e_near, e_pair, 0)
            for o in range(1, n_x):
                far(e_pair, e_far, 0, o).start()
    pair_up(enc_terms, e_near, e_pair, 1)
    for t in range(2):
        enc_chunk(x * 2 + 1 - c, t)
        near(enc_terms, e_near, t, x).start()
    for t in range(2):
        enc_chunk(x * 2 + c, t)
    for o in range(1, n_x):
        far(e_pair, e_far, 0, o).wait_send()
    for o in range(1, n_x):
        far(e_pair, e_far, 1, o).start()
    near(branches, b_near, 2, x).wait_recv()
    added = branches[m].astype(F32) + b_near[x].astype(F32)
    for o in range(1, n_x):
        far(b_pair, b_far, 2, o).wait_recv()
        added = added + b_far[o].astype(F32)
    mixed = (tok[...].astype(F32) + added).astype(BF16)
    mixed_out[...] = mixed
    wide = mixed.astype(F32)
    squares = jnp.broadcast_to(jnp.sum(wide * wide, axis=-1, keepdims=True), (seq_len, 128))
    sq_mine[...] = jnp.transpose(squares)[:8]
    for s in range(1, n_mp):
        sq_copy(s).start()
    def reading_of(holder):
        found = jnp.int32(0)
        for a in range(readings):
            found = jnp.where(picks[a] // own_rows == holder, a, found)
        return found

    finders = [reading_of((d + s) % n_dp) for s in range(n_dp)]
    for t in range(2):
        cols = spans[t]
        near(enc_terms, e_near, t, x).wait_recv()
        total = enc_terms[m, :, :, cols].astype(F32) + e_near[x, :, :, cols].astype(F32)
        for o in range(1, n_x):
            far(e_pair, e_far, t, o).wait_recv()
            total = total + e_far[o, :, :, cols].astype(F32)
        d_norm[:, :, cols] = total.astype(BF16)
        for s in range(1, n_dp):
            holder = (d + s) % n_dp
            back_out[holder, :, cols] = d_norm[finders[s], :, cols]
            back_copy(t, s, holder, d).start()
    back_in[d] = d_norm[finders[0]]
    squares = sq_mine[...]
    for s in range(1, n_mp):
        sq_copy(s).wait_recv()
        squares = squares + sq_all[s]
    squares_out[...] = squares
    for s in range(1, n_dp):
        source = (d + n_dp - s) % n_dp
        for t in range(2):
            back_copy(t, s, source, source).wait_recv()
    for row in range(own_rows):
        rows_out[row] = back_in[askers[row]]
    sent_far(cot_a, 1)
    sent_far(cot_b, 2)
    for t, buf in enumerate((tok_all, cot_a, cot_b, enc_all)):
        sent_near(buf, t)
    for i in range(n_x):
        for t in range(2):
            near(enc_terms, e_near, t, i).wait_send()
        near(branches, b_near, 2, i).wait_send()
    for o in range(1, n_x):
        far(e_pair, e_far, 1, o).wait_send()
        far(b_pair, b_far, 2, o).wait_send()
    for s in range(1, n_dp):
        to = (d + s) % n_dp
        id_copy(s, d).wait_send()
        row_copy(s, to, d).wait_send()
        for t in range(2):
            back_copy(t, s, to, d).wait_send()
    for s in range(1, n_mp):
        sq_copy(s).wait_send()


def finish_kernel(n_mp, mixed, squares, rows, enc, gain_enc, gain_post, mixed_out, ffn_out, denc_out):
    seq_len, feat = mixed.shape
    mixed_out[...] = mixed[...]
    gain_row = row_of(gain_enc)
    scale = jnp.transpose(jnp.broadcast_to(squares[:1], (128, seq_len)))[:, :1]
    scale = lax.rsqrt(scale / (feat * n_mp) + EPS)
    gain = gain_post[lax.axis_index("mp")]
    ffn_out[...] = (mixed[...].astype(F32) * scale * gain).astype(BF16)
    for row in range(enc.shape[0]):
        wide = enc[row].astype(F32)
        scale = rms_scale(wide)
        hat = wide * scale
        up = gain_row * rows[row].astype(F32)
        inner = jnp.mean(up * hat, axis=-1, keepdims=True)
        denc_out[row] = (scale * (up - hat * inner)).astype(BF16)


def shards(
    tokens, cotangent, gain_dec, w_query, w_out, encodings, gain_enc, w_key, w_value, gain_post,
    neighbour_ids,
):
    n_dp, n_mp = lax.axis_size("dp"), lax.axis_size("mp")
    n_x = n_mp // 2
    seq_len, feat = tokens.shape
    head_cols = w_query.shape[1]
    own_rows, share, width = encodings.shape
    blocks = neighbour_ids.shape[0]
    readings = blocks * neighbour_ids.shape[1]
    block = pl.BlockSpec(memory_space=pltpu.VMEM)
    smem = pl.BlockSpec(memory_space=pltpu.SMEM)
    anywhere = pl.BlockSpec(memory_space=pl.ANY)
    dma = pltpu.SemaphoreType.DMA
    shape = jax.ShapeDtypeStruct
    vmem = pltpu.VMEM
    gain_enc = gain_enc.reshape(width // 128, 128)
    tokens_all = vmem((n_mp, seq_len, feat), BF16)
    half_all = vmem((n_mp, seq_len // 2, feat), BF16)
    rows_all = vmem((n_mp, readings, share, width), BF16)
    slots = vmem((n_dp, share, width), BF16)
    local = vmem((seq_len, head_cols), BF16)
    memory = vmem((readings, NLEN, head_cols), BF16)
    rows_x = vmem((n_x, readings, share, width), BF16)
    tokens_x = vmem((n_x, seq_len, feat), BF16)
    mixed, squares, rows = pl.pallas_call(
        functools.partial(layer_kernel, n_dp, n_mp),
        out_shape=(
            shape((seq_len, feat), BF16),
            shape((8, seq_len), F32),
            shape((own_rows, share, width), BF16),
        ),
        in_specs=[block] * 3 + [anywhere] * 2 + [block] * 2 + [anywhere] * 2 + [smem],
        out_specs=(block,) * 3,
        scratch_shapes=[
            tokens_all, half_all, half_all, rows_all, tokens_all,
            vmem((n_mp, feat, head_cols), BF16),
            vmem(w_out.shape, BF16),
            vmem(w_key.shape, BF16),
            vmem(w_value.shape, BF16),
            vmem((own_rows, share, width), F32),
            slots, slots,
            vmem((readings, 128), jnp.int32),
            vmem((n_dp, readings, 128), jnp.int32),
            local, local, memory, memory,
            vmem((blocks, head_cols // HD, BLOCK, NEIGH * NLEN), F32),
            vmem((seq_len, head_cols), F32),
            local, memory, memory,
            rows_all, tokens_all,
            rows_x, rows_x, rows_x, tokens_x, tokens_x, tokens_x,
            vmem((readings, share, width), BF16),
            slots, slots,
            vmem((8, seq_len), F32),
            vmem((n_mp, 8, seq_len), F32),
            dma((4,)),
            dma((4, 2 * n_x)), dma((4, 2 * n_x)),
            dma((n_dp,)), dma((n_dp,)), dma((n_dp,)), dma((n_dp,)),
            dma((3, n_x)), dma((3, n_x)), dma((3, n_x)), dma((3, n_x)),
            dma((2, n_dp)), dma((2, n_dp)), dma((n_mp,)), dma((n_mp,)),
        ],
        compiler_params=pltpu.CompilerParams(
            collective_id=0, has_side_effects=True, vmem_limit_bytes=60 * 1024 * 1024
        ),
        name="layer",
    )(
        tokens, cotangent, gain_dec.reshape(n_mp, 1, feat), w_query.reshape(n_mp, feat, head_cols),
        w_out, encodings, gain_enc, w_key, w_value, neighbour_ids.T,
    )
    return pl.pallas_call(
        functools.partial(finish_kernel, n_mp),
        out_shape=(
            shape((seq_len, feat), BF16),
            shape((seq_len, feat), BF16),
            shape((own_rows, share, width), BF16),
        ),
        in_specs=[block] * 6,
        out_specs=(block,) * 3,
        name="finish",
    )(mixed, squares, rows, encodings, gain_enc, gain_post.reshape(n_mp, 1, feat))


def solution(mesh):
    in_specs = (
        P("dp", "mp"),
        P("dp", "mp"),
        P(),
        P(None, "mp"),
        P("mp", None),
        P("dp", "mp", None),
        P(),
        P(None, "mp"),
        P(None, "mp"),
        P(),
        P("dp", None),
    )
    out_specs = (P("dp", "mp"), P("dp", "mp"), P("dp", "mp", None))
    return jax.shard_map(shards, mesh=mesh, in_specs=in_specs, out_specs=out_specs, check_vma=False)
```

```python
import functools

import jax
import jax.numpy as jnp
from jax import lax
from jax.experimental import pallas as pl
from jax.experimental.pallas import tpu as pltpu
from jax.sharding import PartitionSpec as P

HD = 128
BLOCK = 64
NLEN = 128
NEIGH = 2
LEAD = BLOCK - 1
LOG2_E = 1.4426950408889634
EPS = 1e-06
MESH = pl.DeviceIdType.MESH
BF16 = jnp.bfloat16
F32 = jnp.float32
NT = (((1,), (1,)), ((), ()))
TN = (((0,), (0,)), ((), ()))


def rms_scale(values):
    return lax.rsqrt(jnp.mean(values * values, axis=-1, keepdims=True) + EPS)


def row_of(gain):
    return jnp.concatenate([gain[i : i + 1] for i in range(gain.shape[0])], axis=1)


def place(n_dp, n_mp):
    d, m = lax.axis_index("dp"), lax.axis_index("mp")
    n_x = n_mp // 2
    x, c = m // 2, m % 2
    return d, m, n_x, x, c, x * 2 + (1 - c)


def greet(n_dp, n_mp, d, m):
    barrier = pltpu.get_barrier_semaphore()
    for s in range(1, n_dp):
        pl.semaphore_signal(barrier, inc=1, device_id=((d + s) % n_dp, m), device_id_type=MESH)
    for s in range(1, n_mp):
        pl.semaphore_signal(barrier, inc=1, device_id=(d, (m + s) % n_mp), device_id_type=MESH)
    pl.semaphore_wait(barrier, n_dp + n_mp - 2)


def layer_kernel(
    n_dp, n_mp,
    tok, cot, gain_dec, wq_hbm, wo_hbm, enc, gain_enc, wk_hbm, wv_hbm, chosen,
    mixed_out, squares_out, rows_out,
    tok_all, cot_a, cot_b, enc_all, normed, wq, wo, wk, wv, enc_norm, sending, arrived, ids, idtab,
    q, da, keys, values, prob_all, att, att16, dk, dv,
    enc_terms, branches, e_near, e_pair, e_far, b_near, b_pair, b_far,
    d_norm, back_out, back_in, sq_mine, sq_all,
    w_sem, ag_send, ag_recv, id_send, id_recv, row_send, row_recv,
    near_send, near_recv, far_send, far_recv, back_send, back_recv, sq_send, sq_recv,
):
    d, m, n_x, x, c, partner = place(n_dp, n_mp)
    own_rows, share, width = enc.shape
    readings = ids.shape[0]
    seq_len, feat = tok.shape
    half = seq_len // 2
    head_cols = wq.shape[2]
    heads = head_cols // HD
    factor = HD ** (-0.5)
    cut = (width + 128) // 256 * 128
    spans = (slice(0, cut), slice(cut, width), slice(0, feat))
    loads = [
        pltpu.make_async_copy(a, b, w_sem.at[i])
        for i, (a, b) in enumerate([(wq_hbm, wq), (wo_hbm, wo), (wk_hbm, wk), (wv_hbm, wv)])
    ]
    own = [
        pltpu.make_async_copy(a, b, w_sem.at[4 + i])
        for i, (a, b) in enumerate(
            [
                (tok, tok_all.at[m]),
                (cot.at[pl.ds(0, half)], cot_a.at[m]),
                (cot.at[pl.ds(half, half)], cot_b.at[m]),
            ]
        )
    ]
    for copy in own:
        copy.start()
    for i in (0, 2, 3, 1):
        loads[i].start()

    def hop(buf, t, kind, chunk, target):
        return pltpu.make_async_remote_copy(
            src_ref=buf.at[chunk], dst_ref=buf.at[chunk],
            send_sem=ag_send.at[t, kind], recv_sem=ag_recv.at[t, kind],
            device_id=(d, target), device_id_type=MESH,
        )

    def spread(buf, t):
        for o in range(1, n_x):
            hop(buf, t, o, m, ((x + o) % n_x) * 2 + c).start()
        hop(buf, t, 0, m, partner).start()

    def forward(buf, t):
        for o in range(1, n_x):
            chunk = ((x + n_x - o) % n_x) * 2 + c
            hop(buf, t, o, chunk, partner).wait_recv()
            hop(buf, t, n_x + o, chunk, partner).start()

    def finish(buf, t):
        hop(buf, t, 0, partner, partner).wait_recv()
        for o in range(1, n_x):
            hop(buf, t, n_x + o, ((x + n_x - o) % n_x) * 2 + 1 - c, partner).wait_recv()

    def sent_far(buf, t):
        for o in range(1, n_x):
            hop(buf, t, o, m, partner).wait_send()

    def sent_near(buf, t):
        hop(buf, t, 0, m, partner).wait_send()
        for o in range(1, n_x):
            hop(buf, t, n_x + o, m, partner).wait_send()

    def dp_copy(src, dst, send, recv, s):
        return pltpu.make_async_remote_copy(
            src_ref=src, dst_ref=dst, send_sem=send.at[s], recv_sem=recv.at[s],
            device_id=((d + s) % n_dp, m), device_id_type=MESH,
        )

    def id_copy(s, to):
        return dp_copy(ids, idtab.at[to], id_send, id_recv, s)

    def row_copy(s, src, dst):
        return dp_copy(sending.at[src], arrived.at[dst], row_send, row_recv, s)

    def back_copy(t, s, src, dst):
        cols = spans[t]
        return dp_copy(
            back_out.at[src, :, cols], back_in.at[dst, :, cols],
            back_send.at[t], back_recv.at[t], s,
        )

    def near(buf, land, t, i):
        cols = spans[t]
        return pltpu.make_async_remote_copy(
            src_ref=buf.at[i * 2 + 1 - c, ..., cols], dst_ref=land.at[i, ..., cols],
            send_sem=near_send.at[t, i], recv_sem=near_recv.at[t, i],
            device_id=(d, partner), device_id_type=MESH,
        )

    def far(buf, land, t, o):
        to, cols = (x + o) % n_x, spans[t]
        return pltpu.make_async_remote_copy(
            src_ref=buf.at[to, ..., cols], dst_ref=land.at[o, ..., cols],
            send_sem=far_send.at[t, o], recv_sem=far_recv.at[t, o],
            device_id=(d, to * 2 + c), device_id_type=MESH,
        )

    def sq_copy(s):
        return pltpu.make_async_remote_copy(
            src_ref=sq_mine, dst_ref=sq_all.at[s], send_sem=sq_send.at[s], recv_sem=sq_recv.at[s],
            device_id=(d, (m + s) % n_mp), device_id_type=MESH,
        )

    def pair_up(buf, land, pair, t):
        cols = spans[t]
        for o in range(1, n_x):
            to = (x + o) % n_x
            near(buf, land, t, to).wait_recv()
            theirs = land[to, ..., cols].astype(F32)
            pair[to, ..., cols] = (buf[to * 2 + c, ..., cols].astype(F32) + theirs).astype(BF16)

    picks = [chosen[a % NEIGH, a // NEIGH] for a in range(readings)]
    spot = lax.broadcasted_iota(jnp.int32, (readings, 128), 0)
    listed = jnp.zeros((readings, 128), jnp.int32)
    for a in range(readings):
        listed = jnp.where(spot == a, picks[a], listed)
    ids[...] = listed
    greet(n_dp, n_mp, d, m)
    for s in range(1, n_dp):
        id_copy(s, d).start()
    own[0].wait()
    spread(tok_all, 0)
    idtab[d] = listed
    wide = enc[...].astype(F32)
    enc_norm[...] = wide * rms_scale(wide) * row_of(gain_enc)[None]

    def choose(reader):
        asked = idtab[reader]
        total = jnp.zeros((share, width), F32)
        for row in range(own_rows):
            hit = jnp.where(asked == d * own_rows + row, 1.0, 0.0).astype(F32)
            hit = jnp.max(hit, axis=0, keepdims=True)
            total = total + enc_norm[row] * jnp.concatenate([hit] * (width // 128), axis=1)
        return total.astype(BF16)

    for s in range(1, n_dp):
        reader = (d + s) % n_dp
        id_copy(n_dp - s, reader).wait_recv()
        sending[reader] = choose(reader)
        row_copy(s, reader, d).start()
    arrived[d] = choose(d)
    sent_far(tok_all, 0)
    own[1].wait()
    spread(cot_a, 1)
    forward(tok_all, 0)
    table = idtab[...]
    owner_at = lax.broadcasted_iota(jnp.int32, table.shape, 0)
    askers = [
        jnp.max(jnp.where(table == d * own_rows + row, owner_at, 0)) for row in range(own_rows)
    ]
    for s in range(1, n_dp):
        holder = (d + n_dp - s) % n_dp
        row_copy(s, holder, holder).wait_recv()
    for a in range(readings):
        enc_all[m, a] = arrived[picks[a] // own_rows]
    spread(enc_all, 3)
    finish(tok_all, 0)
    squares = jnp.zeros((seq_len, 1), F32)
    for k in range(n_mp):
        part = tok_all[k].astype(F32)
        squares = squares + jnp.sum(part * part, axis=-1, keepdims=True)
    scale = lax.rsqrt(squares / (feat * n_mp) + EPS)
    for k in range(n_mp):
        normed[k] = (tok_all[k].astype(F32) * scale * gain_dec[k]).astype(BF16)
    loads[0].wait()
    keep = lax.broadcasted_iota(jnp.int32, (seq_len, 256), 0) < seq_len - LEAD

    def shift_up(part):
        return jnp.where(keep, pltpu.roll(part, seq_len - LEAD, 0), 0.0).astype(BF16)

    def query_tile(n, _):
        cols = pl.ds(pl.multiple_of(n * 256, 256), 256)
        acc = jnp.zeros((seq_len, 256), F32)
        for k in range(n_mp):
            acc += jnp.dot(normed[k], wq[k, :, cols], preferred_element_type=F32)
        q[:, cols] = shift_up(acc)
        return 0

    lax.fori_loop(0, head_cols // 256, query_tile, 0)
    forward(cot_a, 1)
    sent_far(enc_all, 3)
    own[2].wait()
    spread(cot_b, 2)
    loads[2].wait()
    loads[3].wait()

    def project_memory(k):
        toks = pl.ds(pl.multiple_of(k * share, share), share)
        rows = enc_all[k].reshape(readings * share, width)

        def tile(n, _):
            cols = pl.ds(pl.multiple_of(n * 256, 256), 256)
            for weight, out in ((wk, keys), (wv, values)):
                part = jnp.dot(rows, weight[:, cols], preferred_element_type=F32).astype(BF16)
                out[:, toks, cols] = part.reshape(readings, share, 256)
            return 0

        lax.fori_loop(0, head_cols // 256, tile, 0)

    project_memory(m)
    hop(enc_all, 3, 0, partner, partner).wait_recv()
    project_memory(partner)
    forward(enc_all, 3)
    for o in range(1, n_x):
        project_memory(((x + n_x - o) % n_x) * 2 + c)
    for o in range(1, n_x):
        chunk = ((x + n_x - o) % n_x) * 2 + 1 - c
        hop(enc_all, 3, n_x + o, chunk, partner).wait_recv()
        project_memory(chunk)

    def memory_of(buf, b, h):
        part = buf[pl.ds(b * NEIGH, NEIGH), :, h * HD : (h + 1) * HD]
        return part.reshape(NEIGH * NLEN, HD)

    def attend(b, _):
        rows = pl.ds(pl.multiple_of(b * BLOCK, BLOCK), BLOCK)
        for h0 in range(0, heads, 8):
            group = range(h0, min(h0 + 8, heads))
            scores = [
                lax.dot_general(
                    q[rows, h * HD : (h + 1) * HD], memory_of(keys, b, h), NT,
                    preferred_element_type=F32,
                )
                for h in group
            ]
            lifted = [
                jnp.exp2((v - jnp.max(v, axis=-1, keepdims=True)) * (factor * LOG2_E)) for v in scores
            ]
            prob = [v * (1.0 / jnp.sum(v, axis=-1, keepdims=True)) for v in lifted]
            for h, v in zip(group, prob):
                prob_all[b, h] = v
            for h, v in zip(group, prob):
                att[rows, h * HD : (h + 1) * HD] = jnp.dot(
                    v.astype(BF16), memory_of(values, b, h), preferred_element_type=F32
                )
        return 0

    lax.fori_loop(0, seq_len // BLOCK, attend, 0)
    low = lax.broadcasted_iota(jnp.int32, (seq_len, head_cols), 0) >= LEAD
    att16[...] = jnp.where(low, pltpu.roll(att[...], LEAD, 0), 0.0).astype(BF16)
    loads[1].wait()

    def branch_chunk(k, _):
        cols = pl.ds(pl.multiple_of(k * feat, feat), feat)
        branches[k] = jnp.dot(att16[...], wo[:, cols], preferred_element_type=F32).astype(BF16)
        return 0

    lax.fori_loop(0, n_mp, branch_chunk, 0)
    for i in range(n_x):
        near(branches, b_near, 2, i).start()
    forward(cot_b, 2)
    pair_up(branches, b_near, b_pair, 2)
    for o in range(1, n_x):
        far(b_pair, b_far, 2, o).start()
    finish(cot_a, 1)
    finish(cot_b, 2)

    def grad_tile(n, _):
        cols = pl.ds(pl.multiple_of(n * 256, 256), 256)
        acc = jnp.zeros((seq_len, 256), F32)
        for k in range(n_mp):
            acc += lax.dot_general(
                jnp.concatenate([cot_a[k], cot_b[k]], axis=0),
                wo[cols, k * feat : (k + 1) * feat], NT, preferred_element_type=F32,
            )
        da[:, cols] = shift_up(acc)
        return 0

    lax.fori_loop(0, head_cols // 256, grad_tile, 0)

    def attend_back(b, _):
        rows = pl.ds(pl.multiple_of(b * BLOCK, BLOCK), BLOCK)
        mem = pl.ds(b * NEIGH, NEIGH)
        for h0 in range(0, heads, 8):
            group = range(h0, min(h0 + 8, heads))
            d_prob = [
                lax.dot_general(
                    da[rows, h * HD : (h + 1) * HD], memory_of(values, b, h), NT,
                    preferred_element_type=F32,
                )
                for h in group
            ]
            for h in group:
                cols = slice(h * HD, (h + 1) * HD)
                dv_h = lax.dot_general(
                    prob_all[b, h].astype(BF16), da[rows, cols], TN, preferred_element_type=F32
                )
                dv[mem, :, cols] = dv_h.astype(BF16).reshape(NEIGH, NLEN, HD)
            d_scores = []
            for h, v in zip(group, d_prob):
                prob = prob_all[b, h]
                inner = jnp.sum(prob * v, axis=-1, keepdims=True)
                d_scores.append((prob * (v - inner) * factor).astype(BF16))
            for h, v in zip(group, d_scores):
                cols = slice(h * HD, (h + 1) * HD)
                dk_h = lax.dot_general(v, q[rows, cols], TN, preferred_element_type=F32)
                dk[mem, :, cols] = dk_h.astype(BF16).reshape(NEIGH, NLEN, HD)
        return 0

    lax.fori_loop(0, seq_len // BLOCK, attend_back, 0)

    def enc_chunk(k, t):
        toks = pl.ds(pl.multiple_of(k * share, share), share)
        cols = spans[t]
        acc = lax.dot_general(
            dk[:, toks, :].reshape(readings * share, head_cols), wk[cols, :], NT,
            preferred_element_type=F32,
        )
        acc += lax.dot_general(
            dv[:, toks, :].reshape(readings * share, head_cols), wv[cols, :], NT,
            preferred_element_type=F32,
        )
        enc_terms[k, :, :, cols] = acc.astype(BF16).reshape(readings, share, cols.stop - cols.start)

    for t in range(2):
        for o in range(1, n_x):
            to = (x + o) % n_x
            enc_chunk(to * 2 + 1 - c, t)
            near(enc_terms, e_near, t, to).start()
        for o in range(1, n_x):
            enc_chunk((x + o) % n_x * 2 + c, t)
        if t == 0:
            pair_up(enc_terms, e_near, e_pair, 0)
            for o in range(1, n_x):
                far(e_pair, e_far, 0, o).start()
    pair_up(enc_terms, e_near, e_pair, 1)
    for t in range(2):
        enc_chunk(x * 2 + 1 - c, t)
        near(enc_terms, e_near, t, x).start()
    for t in range(2):
        enc_chunk(x * 2 + c, t)
    for o in range(1, n_x):
        far(e_pair, e_far, 0, o).wait_send()
    for o in range(1, n_x):
        far(e_pair, e_far, 1, o).start()
    near(branches, b_near, 2, x).wait_recv()
    added = branches[m].astype(F32) + b_near[x].astype(F32)
    for o in range(1, n_x):
        far(b_pair, b_far, 2, o).wait_recv()
        added = added + b_far[o].astype(F32)
    mixed = (tok_all[m].astype(F32) + added).astype(BF16)
    mixed_out[...] = mixed
    wide = mixed.astype(F32)
    squares = jnp.broadcast_to(jnp.sum(wide * wide, axis=-1, keepdims=True), (seq_len, 128))
    sq_mine[...] = jnp.transpose(squares)[:8]
    for s in range(1, n_mp):
        sq_copy(s).start()
    def reading_of(holder):
        found = jnp.int32(0)
        for a in range(readings):
            found = jnp.where(picks[a] // own_rows == holder, a, found)
        return found

    finders = [reading_of((d + s) % n_dp) for s in range(n_dp)]
    for t in range(2):
        cols = spans[t]
        near(enc_terms, e_near, t, x).wait_recv()
        total = enc_terms[m, :, :, cols].astype(F32) + e_near[x, :, :, cols].astype(F32)
        for o in range(1, n_x):
            far(e_pair, e_far, t, o).wait_recv()
            total = total + e_far[o, :, :, cols].astype(F32)
        d_norm[:, :, cols] = total.astype(BF16)
        for s in range(1, n_dp):
            holder = (d + s) % n_dp
            back_out[holder, :, cols] = d_norm[finders[s], :, cols]
            back_copy(t, s, holder, d).start()
    back_in[d] = d_norm[finders[0]]
    squares = sq_mine[...]
    for s in range(1, n_mp):
        sq_copy(s).wait_recv()
        squares = squares + sq_all[s]
    squares_out[...] = squares
    for s in range(1, n_dp):
        source = (d + n_dp - s) % n_dp
        for t in range(2):
            back_copy(t, s, source, source).wait_recv()
    for row in range(own_rows):
        rows_out[row] = back_in[askers[row]]
    sent_far(cot_a, 1)
    sent_far(cot_b, 2)
    for t, buf in enumerate((tok_all, cot_a, cot_b, enc_all)):
        sent_near(buf, t)
    for i in range(n_x):
        for t in range(2):
            near(enc_terms, e_near, t, i).wait_send()
        near(branches, b_near, 2, i).wait_send()
    for o in range(1, n_x):
        far(e_pair, e_far, 1, o).wait_send()
        far(b_pair, b_far, 2, o).wait_send()
    for s in range(1, n_dp):
        to = (d + s) % n_dp
        id_copy(s, d).wait_send()
        row_copy(s, to, d).wait_send()
        for t in range(2):
            back_copy(t, s, to, d).wait_send()
    for s in range(1, n_mp):
        sq_copy(s).wait_send()


def finish_kernel(n_mp, mixed, squares, rows, enc, gain_enc, gain_post, mixed_out, ffn_out, denc_out):
    seq_len, feat = mixed.shape
    mixed_out[...] = mixed[...]
    gain_row = row_of(gain_enc)
    scale = jnp.transpose(jnp.broadcast_to(squares[:1], (128, seq_len)))[:, :1]
    scale = lax.rsqrt(scale / (feat * n_mp) + EPS)
    gain = gain_post[lax.axis_index("mp")]
    ffn_out[...] = (mixed[...].astype(F32) * scale * gain).astype(BF16)
    for row in range(enc.shape[0]):
        wide = enc[row].astype(F32)
        scale = rms_scale(wide)
        hat = wide * scale
        up = gain_row * rows[row].astype(F32)
        inner = jnp.mean(up * hat, axis=-1, keepdims=True)
        denc_out[row] = (scale * (up - hat * inner)).astype(BF16)


def shards(
    tokens, cotangent, gain_dec, w_query, w_out, encodings, gain_enc, w_key, w_value, gain_post,
    neighbour_ids,
):
    n_dp, n_mp = lax.axis_size("dp"), lax.axis_size("mp")
    n_x = n_mp // 2
    seq_len, feat = tokens.shape
    head_cols = w_query.shape[1]
    own_rows, share, width = encodings.shape
    blocks = neighbour_ids.shape[0]
    readings = blocks * neighbour_ids.shape[1]
    block = pl.BlockSpec(memory_space=pltpu.VMEM)
    smem = pl.BlockSpec(memory_space=pltpu.SMEM)
    anywhere = pl.BlockSpec(memory_space=pl.ANY)
    dma = pltpu.SemaphoreType.DMA
    shape = jax.ShapeDtypeStruct
    vmem = pltpu.VMEM
    gain_enc = gain_enc.reshape(width // 128, 128)
    tokens_all = vmem((n_mp, seq_len, feat), BF16)
    half_all = vmem((n_mp, seq_len // 2, feat), BF16)
    rows_all = vmem((n_mp, readings, share, width), BF16)
    slots = vmem((n_dp, share, width), BF16)
    local = vmem((seq_len, head_cols), BF16)
    memory = vmem((readings, NLEN, head_cols), BF16)
    rows_x = vmem((n_x, readings, share, width), BF16)
    tokens_x = vmem((n_x, seq_len, feat), BF16)
    mixed, squares, rows = pl.pallas_call(
        functools.partial(layer_kernel, n_dp, n_mp),
        out_shape=(
            shape((seq_len, feat), BF16),
            shape((8, seq_len), F32),
            shape((own_rows, share, width), BF16),
        ),
        in_specs=[anywhere] * 2 + [block] + [anywhere] * 2 + [block] * 2 + [anywhere] * 2 + [smem],
        out_specs=(block,) * 3,
        scratch_shapes=[
            tokens_all, half_all, half_all, rows_all, tokens_all,
            vmem((n_mp, feat, head_cols), BF16),
            vmem(w_out.shape, BF16),
            vmem(w_key.shape, BF16),
            vmem(w_value.shape, BF16),
            vmem((own_rows, share, width), F32),
            slots, slots,
            vmem((readings, 128), jnp.int32),
            vmem((n_dp, readings, 128), jnp.int32),
            local, local, memory, memory,
            vmem((blocks, head_cols // HD, BLOCK, NEIGH * NLEN), F32),
            vmem((seq_len, head_cols), F32),
            local, memory, memory,
            rows_all, tokens_all,
            rows_x, rows_x, rows_x, tokens_x, tokens_x, tokens_x,
            vmem((readings, share, width), BF16),
            slots, slots,
            vmem((8, seq_len), F32),
            vmem((n_mp, 8, seq_len), F32),
            dma((7,)),
            dma((4, 2 * n_x)), dma((4, 2 * n_x)),
            dma((n_dp,)), dma((n_dp,)), dma((n_dp,)), dma((n_dp,)),
            dma((3, n_x)), dma((3, n_x)), dma((3, n_x)), dma((3, n_x)),
            dma((2, n_dp)), dma((2, n_dp)), dma((n_mp,)), dma((n_mp,)),
        ],
        compiler_params=pltpu.CompilerParams(
            collective_id=0, has_side_effects=True, vmem_limit_bytes=60 * 1024 * 1024
        ),
        name="layer",
    )(
        tokens, cotangent, gain_dec.reshape(n_mp, 1, feat), w_query.reshape(n_mp, feat, head_cols),
        w_out, encodings, gain_enc, w_key, w_value, neighbour_ids.T,
    )
    return pl.pallas_call(
        functools.partial(finish_kernel, n_mp),
        out_shape=(
            shape((seq_len, feat), BF16),
            shape((seq_len, feat), BF16),
            shape((own_rows, share, width), BF16),
        ),
        in_specs=[block] * 6,
        out_specs=(block,) * 3,
        name="finish",
    )(mixed, squares, rows, encodings, gain_enc, gain_post.reshape(n_mp, 1, feat))


def solution(mesh):
    in_specs = (
        P("dp", "mp"),
        P("dp", "mp"),
        P(),
        P(None, "mp"),
        P("mp", None),
        P("dp", "mp", None),
        P(),
        P(None, "mp"),
        P(None, "mp"),
        P(),
        P("dp", None),
    )
    out_specs = (P("dp", "mp"), P("dp", "mp"), P("dp", "mp", None))
    return jax.shard_map(shards, mesh=mesh, in_specs=in_specs, out_specs=out_specs, check_vma=False)
```

```python
import functools

import jax
import jax.numpy as jnp
from jax import lax
from jax.experimental import pallas as pl
from jax.experimental.pallas import tpu as pltpu
from jax.sharding import PartitionSpec as P

HD = 128
BLOCK = 64
NLEN = 128
NEIGH = 2
LEAD = BLOCK - 1
LOG2_E = 1.4426950408889634
EPS = 1e-06
MESH = pl.DeviceIdType.MESH
BF16 = jnp.bfloat16
F32 = jnp.float32
NT = (((1,), (1,)), ((), ()))
TN = (((0,), (0,)), ((), ()))


def rms_scale(values):
    return lax.rsqrt(jnp.mean(values * values, axis=-1, keepdims=True) + EPS)


def row_of(gain):
    return jnp.concatenate([gain[i : i + 1] for i in range(gain.shape[0])], axis=1)


def place(n_dp, n_mp):
    d, m = lax.axis_index("dp"), lax.axis_index("mp")
    n_x = n_mp // 2
    x, c = m // 2, m % 2
    return d, m, n_x, x, c, x * 2 + (1 - c)


def greet(n_dp, n_mp, d, m):
    barrier = pltpu.get_barrier_semaphore()
    for s in range(1, n_dp):
        pl.semaphore_signal(barrier, inc=1, device_id=((d + s) % n_dp, m), device_id_type=MESH)
    for s in range(1, n_mp):
        pl.semaphore_signal(barrier, inc=1, device_id=(d, (m + s) % n_mp), device_id_type=MESH)
    pl.semaphore_wait(barrier, n_dp + n_mp - 2)


def layer_kernel(
    n_dp, n_mp,
    tok, cot, gain_dec, wq_hbm, wo_hbm, enc, gain_enc, wk_hbm, wv_hbm, chosen,
    mixed_out, squares_out, rows_out,
    tok_all, cot_a, cot_b, enc_all, normed, wq, wo, wk, wv, enc_norm, sending, arrived, ids, idtab,
    q, da, keys, values, prob_all, att, att16, dk, dv,
    enc_terms, branches, e_near, e_pair, e_far, b_near, b_pair, b_far,
    d_norm, back_out, back_in, sq_mine, sq_all,
    w_sem, ag_send, ag_recv, id_send, id_recv, row_send, row_recv,
    near_send, near_recv, far_send, far_recv, back_send, back_recv, sq_send, sq_recv,
):
    d, m, n_x, x, c, partner = place(n_dp, n_mp)
    own_rows, share, width = enc.shape
    readings = ids.shape[0]
    seq_len, feat = tok.shape
    half = seq_len // 2
    head_cols = wq.shape[2]
    heads = head_cols // HD
    factor = HD ** (-0.5)
    cut = width // 256 * 128
    spans = (slice(0, cut), slice(cut, width), slice(0, feat))
    loads = [
        pltpu.make_async_copy(a, b, w_sem.at[i])
        for i, (a, b) in enumerate([(wq_hbm, wq), (wo_hbm, wo), (wk_hbm, wk), (wv_hbm, wv)])
    ]
    own = [
        pltpu.make_async_copy(a, b, w_sem.at[4 + i])
        for i, (a, b) in enumerate(
            [
                (tok, tok_all.at[m]),
                (cot.at[pl.ds(0, half)], cot_a.at[m]),
                (cot.at[pl.ds(half, half)], cot_b.at[m]),
            ]
        )
    ]
    for copy in own:
        copy.start()
    for i in (0, 2, 3, 1):
        loads[i].start()

    def hop(buf, t, kind, chunk, target):
        return pltpu.make_async_remote_copy(
            src_ref=buf.at[chunk], dst_ref=buf.at[chunk],
            send_sem=ag_send.at[t, kind], recv_sem=ag_recv.at[t, kind],
            device_id=(d, target), device_id_type=MESH,
        )

    def spread(buf, t):
        for o in range(1, n_x):
            hop(buf, t, o, m, ((x + o) % n_x) * 2 + c).start()
        hop(buf, t, 0, m, partner).start()

    def forward(buf, t):
        for o in range(1, n_x):
            chunk = ((x + n_x - o) % n_x) * 2 + c
            hop(buf, t, o, chunk, partner).wait_recv()
            hop(buf, t, n_x + o, chunk, partner).start()

    def finish(buf, t):
        hop(buf, t, 0, partner, partner).wait_recv()
        for o in range(1, n_x):
            hop(buf, t, n_x + o, ((x + n_x - o) % n_x) * 2 + 1 - c, partner).wait_recv()

    def sent_far(buf, t):
        for o in range(1, n_x):
            hop(buf, t, o, m, partner).wait_send()

    def sent_near(buf, t):
        hop(buf, t, 0, m, partner).wait_send()
        for o in range(1, n_x):
            hop(buf, t, n_x + o, m, partner).wait_send()

    def dp_copy(src, dst, send, recv, s):
        return pltpu.make_async_remote_copy(
            src_ref=src, dst_ref=dst, send_sem=send.at[s], recv_sem=recv.at[s],
            device_id=((d + s) % n_dp, m), device_id_type=MESH,
        )

    def id_copy(s, to):
        return dp_copy(ids, idtab.at[to], id_send, id_recv, s)

    def row_copy(s, src, dst):
        return dp_copy(sending.at[src], arrived.at[dst], row_send, row_recv, s)

    def back_copy(t, s, src, dst):
        cols = spans[t]
        return dp_copy(
            back_out.at[src, :, cols], back_in.at[dst, :, cols],
            back_send.at[t], back_recv.at[t], s,
        )

    def near(buf, land, t, i):
        cols = spans[t]
        return pltpu.make_async_remote_copy(
            src_ref=buf.at[i * 2 + 1 - c, ..., cols], dst_ref=land.at[i, ..., cols],
            send_sem=near_send.at[t, i], recv_sem=near_recv.at[t, i],
            device_id=(d, partner), device_id_type=MESH,
        )

    def far(buf, land, t, o):
        to, cols = (x + o) % n_x, spans[t]
        return pltpu.make_async_remote_copy(
            src_ref=buf.at[to, ..., cols], dst_ref=land.at[o, ..., cols],
            send_sem=far_send.at[t, o], recv_sem=far_recv.at[t, o],
            device_id=(d, to * 2 + c), device_id_type=MESH,
        )

    def sq_copy(s):
        return pltpu.make_async_remote_copy(
            src_ref=sq_mine, dst_ref=sq_all.at[s], send_sem=sq_send.at[s], recv_sem=sq_recv.at[s],
            device_id=(d, (m + s) % n_mp), device_id_type=MESH,
        )

    def pair_up(buf, land, pair, t):
        cols = spans[t]
        for o in range(1, n_x):
            to = (x + o) % n_x
            near(buf, land, t, to).wait_recv()
            theirs = land[to, ..., cols].astype(F32)
            pair[to, ..., cols] = (buf[to * 2 + c, ..., cols].astype(F32) + theirs).astype(BF16)

    picks = [chosen[a % NEIGH, a // NEIGH] for a in range(readings)]
    spot = lax.broadcasted_iota(jnp.int32, (readings, 128), 0)
    listed = jnp.zeros((readings, 128), jnp.int32)
    for a in range(readings):
        listed = jnp.where(spot == a, picks[a], listed)
    ids[...] = listed
    greet(n_dp, n_mp, d, m)
    for s in range(1, n_dp):
        id_copy(s, d).start()
    own[0].wait()
    spread(tok_all, 0)
    idtab[d] = listed
    wide = enc[...].astype(F32)
    enc_norm[...] = wide * rms_scale(wide) * row_of(gain_enc)[None]

    def choose(reader):
        asked = idtab[reader]
        total = jnp.zeros((share, width), F32)
        for row in range(own_rows):
            hit = jnp.where(asked == d * own_rows + row, 1.0, 0.0).astype(F32)
            hit = jnp.max(hit, axis=0, keepdims=True)
            total = total + enc_norm[row] * jnp.concatenate([hit] * (width // 128), axis=1)
        return total.astype(BF16)

    for s in range(1, n_dp):
        reader = (d + s) % n_dp
        id_copy(n_dp - s, reader).wait_recv()
        sending[reader] = choose(reader)
        row_copy(s, reader, d).start()
    arrived[d] = choose(d)
    sent_far(tok_all, 0)
    forward(tok_all, 0)
    table = idtab[...]
    owner_at = lax.broadcasted_iota(jnp.int32, table.shape, 0)
    askers = [
        jnp.max(jnp.where(table == d * own_rows + row, owner_at, 0)) for row in range(own_rows)
    ]
    for s in range(1, n_dp):
        holder = (d + n_dp - s) % n_dp
        row_copy(s, holder, holder).wait_recv()
    for a in range(readings):
        enc_all[m, a] = arrived[picks[a] // own_rows]
    spread(enc_all, 3)
    finish(tok_all, 0)
    squares = jnp.zeros((seq_len, 1), F32)
    for k in range(n_mp):
        part = tok_all[k].astype(F32)
        squares = squares + jnp.sum(part * part, axis=-1, keepdims=True)
    scale = lax.rsqrt(squares / (feat * n_mp) + EPS)
    for k in range(n_mp):
        normed[k] = (tok_all[k].astype(F32) * scale * gain_dec[k]).astype(BF16)
    loads[0].wait()
    keep = lax.broadcasted_iota(jnp.int32, (seq_len, 256), 0) < seq_len - LEAD

    def shift_up(part):
        return jnp.where(keep, pltpu.roll(part, seq_len - LEAD, 0), 0.0).astype(BF16)

    def query_tile(n, _):
        cols = pl.ds(pl.multiple_of(n * 256, 256), 256)
        acc = jnp.zeros((seq_len, 256), F32)
        for k in range(n_mp):
            acc += jnp.dot(normed[k], wq[k, :, cols], preferred_element_type=F32)
        q[:, cols] = shift_up(acc)
        return 0

    lax.fori_loop(0, head_cols // 256, query_tile, 0)
    sent_far(enc_all, 3)
    own[1].wait()
    spread(cot_a, 1)
    own[2].wait()
    spread(cot_b, 2)
    loads[2].wait()
    loads[3].wait()

    def project_memory(k):
        toks = pl.ds(pl.multiple_of(k * share, share), share)
        rows = enc_all[k].reshape(readings * share, width)

        def tile(n, _):
            cols = pl.ds(pl.multiple_of(n * 256, 256), 256)
            for weight, out in ((wk, keys), (wv, values)):
                part = jnp.dot(rows, weight[:, cols], preferred_element_type=F32).astype(BF16)
                out[:, toks, cols] = part.reshape(readings, share, 256)
            return 0

        lax.fori_loop(0, head_cols // 256, tile, 0)

    project_memory(m)
    hop(enc_all, 3, 0, partner, partner).wait_recv()
    project_memory(partner)
    forward(enc_all, 3)
    for o in range(1, n_x):
        project_memory(((x + n_x - o) % n_x) * 2 + c)
    for o in range(1, n_x):
        chunk = ((x + n_x - o) % n_x) * 2 + 1 - c
        hop(enc_all, 3, n_x + o, chunk, partner).wait_recv()
        project_memory(chunk)
    forward(cot_a, 1)

    def memory_of(buf, b, h):
        part = buf[pl.ds(b * NEIGH, NEIGH), :, h * HD : (h + 1) * HD]
        return part.reshape(NEIGH * NLEN, HD)

    def attend(b, _):
        rows = pl.ds(pl.multiple_of(b * BLOCK, BLOCK), BLOCK)
        for h0 in range(0, heads, 8):
            group = range(h0, min(h0 + 8, heads))
            scores = [
                lax.dot_general(
                    q[rows, h * HD : (h + 1) * HD], memory_of(keys, b, h), NT,
                    preferred_element_type=F32,
                )
                for h in group
            ]
            lifted = [
                jnp.exp2((v - jnp.max(v, axis=-1, keepdims=True)) * (factor * LOG2_E)) for v in scores
            ]
            prob = [v * (1.0 / jnp.sum(v, axis=-1, keepdims=True)) for v in lifted]
            for h, v in zip(group, prob):
                prob_all[b, h] = v
            for h, v in zip(group, prob):
                att[rows, h * HD : (h + 1) * HD] = jnp.dot(
                    v.astype(BF16), memory_of(values, b, h), preferred_element_type=F32
                )
        return 0

    lax.fori_loop(0, seq_len // BLOCK, attend, 0)
    low = lax.broadcasted_iota(jnp.int32, (seq_len, head_cols), 0) >= LEAD
    att16[...] = jnp.where(low, pltpu.roll(att[...], LEAD, 0), 0.0).astype(BF16)
    loads[1].wait()

    def branch_chunk(k, _):
        cols = pl.ds(pl.multiple_of(k * feat, feat), feat)
        branches[k] = jnp.dot(att16[...], wo[:, cols], preferred_element_type=F32).astype(BF16)
        return 0

    lax.fori_loop(0, n_mp, branch_chunk, 0)
    for i in range(n_x):
        near(branches, b_near, 2, i).start()
    forward(cot_b, 2)
    pair_up(branches, b_near, b_pair, 2)
    for o in range(1, n_x):
        far(b_pair, b_far, 2, o).start()
    finish(cot_a, 1)
    finish(cot_b, 2)

    def grad_tile(n, _):
        cols = pl.ds(pl.multiple_of(n * 256, 256), 256)
        acc = jnp.zeros((seq_len, 256), F32)
        for k in range(n_mp):
            acc += lax.dot_general(
                jnp.concatenate([cot_a[k], cot_b[k]], axis=0),
                wo[cols, k * feat : (k + 1) * feat], NT, preferred_element_type=F32,
            )
        da[:, cols] = shift_up(acc)
        return 0

    lax.fori_loop(0, head_cols // 256, grad_tile, 0)

    def attend_back(b, _):
        rows = pl.ds(pl.multiple_of(b * BLOCK, BLOCK), BLOCK)
        mem = pl.ds(b * NEIGH, NEIGH)
        for h0 in range(0, heads, 8):
            group = range(h0, min(h0 + 8, heads))
            d_prob = [
                lax.dot_general(
                    da[rows, h * HD : (h + 1) * HD], memory_of(values, b, h), NT,
                    preferred_element_type=F32,
                )
                for h in group
            ]
            for h in group:
                cols = slice(h * HD, (h + 1) * HD)
                dv_h = lax.dot_general(
                    prob_all[b, h].astype(BF16), da[rows, cols], TN, preferred_element_type=F32
                )
                dv[mem, :, cols] = dv_h.astype(BF16).reshape(NEIGH, NLEN, HD)
            d_scores = []
            for h, v in zip(group, d_prob):
                prob = prob_all[b, h]
                inner = jnp.sum(prob * v, axis=-1, keepdims=True)
                d_scores.append((prob * (v - inner) * factor).astype(BF16))
            for h, v in zip(group, d_scores):
                cols = slice(h * HD, (h + 1) * HD)
                dk_h = lax.dot_general(v, q[rows, cols], TN, preferred_element_type=F32)
                dk[mem, :, cols] = dk_h.astype(BF16).reshape(NEIGH, NLEN, HD)
        return 0

    lax.fori_loop(0, seq_len // BLOCK, attend_back, 0)

    def enc_chunk(k, t):
        toks = pl.ds(pl.multiple_of(k * share, share), share)
        cols = spans[t]
        acc = lax.dot_general(
            dk[:, toks, :].reshape(readings * share, head_cols), wk[cols, :], NT,
            preferred_element_type=F32,
        )
        acc += lax.dot_general(
            dv[:, toks, :].reshape(readings * share, head_cols), wv[cols, :], NT,
            preferred_element_type=F32,
        )
        enc_terms[k, :, :, cols] = acc.astype(BF16).reshape(readings, share, cols.stop - cols.start)

    for t in range(2):
        for o in range(1, n_x):
            to = (x + o) % n_x
            enc_chunk(to * 2 + 1 - c, t)
            near(enc_terms, e_near, t, to).start()
        for o in range(1, n_x):
            enc_chunk((x + o) % n_x * 2 + c, t)
        if t == 0:
            pair_up(enc_terms, e_near, e_pair, 0)
            for o in range(1, n_x):
                far(e_pair, e_far, 0, o).start()
    pair_up(enc_terms, e_near, e_pair, 1)
    for t in range(2):
        enc_chunk(x * 2 + 1 - c, t)
        near(enc_terms, e_near, t, x).start()
    for t in range(2):
        enc_chunk(x * 2 + c, t)
    for o in range(1, n_x):
        far(e_pair, e_far, 0, o).wait_send()
    for o in range(1, n_x):
        far(e_pair, e_far, 1, o).start()
    near(branches, b_near, 2, x).wait_recv()
    added = branches[m].astype(F32) + b_near[x].astype(F32)
    for o in range(1, n_x):
        far(b_pair, b_far, 2, o).wait_recv()
        added = added + b_far[o].astype(F32)
    mixed = (tok_all[m].astype(F32) + added).astype(BF16)
    mixed_out[...] = mixed
    wide = mixed.astype(F32)
    squares = jnp.broadcast_to(jnp.sum(wide * wide, axis=-1, keepdims=True), (seq_len, 128))
    sq_mine[...] = jnp.transpose(squares)[:8]
    for s in range(1, n_mp):
        sq_copy(s).start()
    def reading_of(holder):
        found = jnp.int32(0)
        for a in range(readings):
            found = jnp.where(picks[a] // own_rows == holder, a, found)
        return found

    finders = [reading_of((d + s) % n_dp) for s in range(n_dp)]
    for t in range(2):
        cols = spans[t]
        near(enc_terms, e_near, t, x).wait_recv()
        total = enc_terms[m, :, :, cols].astype(F32) + e_near[x, :, :, cols].astype(F32)
        for o in range(1, n_x):
            far(e_pair, e_far, t, o).wait_recv()
            total = total + e_far[o, :, :, cols].astype(F32)
        d_norm[:, :, cols] = total.astype(BF16)
        for s in range(1, n_dp):
            holder = (d + s) % n_dp
            back_out[holder, :, cols] = d_norm[finders[s], :, cols]
            back_copy(t, s, holder, d).start()
    back_in[d] = d_norm[finders[0]]
    squares = sq_mine[...]
    for s in range(1, n_mp):
        sq_copy(s).wait_recv()
        squares = squares + sq_all[s]
    squares_out[...] = squares
    for s in range(1, n_dp):
        source = (d + n_dp - s) % n_dp
        for t in range(2):
            back_copy(t, s, source, source).wait_recv()
    for row in range(own_rows):
        rows_out[row] = back_in[askers[row]]
    sent_far(cot_a, 1)
    sent_far(cot_b, 2)
    for t, buf in enumerate((tok_all, cot_a, cot_b, enc_all)):
        sent_near(buf, t)
    for i in range(n_x):
        for t in range(2):
            near(enc_terms, e_near, t, i).wait_send()
        near(branches, b_near, 2, i).wait_send()
    for o in range(1, n_x):
        far(e_pair, e_far, 1, o).wait_send()
        far(b_pair, b_far, 2, o).wait_send()
    for s in range(1, n_dp):
        to = (d + s) % n_dp
        id_copy(s, d).wait_send()
        row_copy(s, to, d).wait_send()
        for t in range(2):
            back_copy(t, s, to, d).wait_send()
    for s in range(1, n_mp):
        sq_copy(s).wait_send()


def finish_kernel(n_mp, mixed, squares, rows, enc, gain_enc, gain_post, mixed_out, ffn_out, denc_out):
    seq_len, feat = mixed.shape
    mixed_out[...] = mixed[...]
    gain_row = row_of(gain_enc)
    scale = jnp.transpose(jnp.broadcast_to(squares[:1], (128, seq_len)))[:, :1]
    scale = lax.rsqrt(scale / (feat * n_mp) + EPS)
    gain = gain_post[lax.axis_index("mp")]
    ffn_out[...] = (mixed[...].astype(F32) * scale * gain).astype(BF16)
    for row in range(enc.shape[0]):
        wide = enc[row].astype(F32)
        scale = rms_scale(wide)
        hat = wide * scale
        up = gain_row * rows[row].astype(F32)
        inner = jnp.mean(up * hat, axis=-1, keepdims=True)
        denc_out[row] = (scale * (up - hat * inner)).astype(BF16)


def shards(
    tokens, cotangent, gain_dec, w_query, w_out, encodings, gain_enc, w_key, w_value, gain_post,
    neighbour_ids,
):
    n_dp, n_mp = lax.axis_size("dp"), lax.axis_size("mp")
    n_x = n_mp // 2
    seq_len, feat = tokens.shape
    head_cols = w_query.shape[1]
    own_rows, share, width = encodings.shape
    blocks = neighbour_ids.shape[0]
    readings = blocks * neighbour_ids.shape[1]
    block = pl.BlockSpec(memory_space=pltpu.VMEM)
    smem = pl.BlockSpec(memory_space=pltpu.SMEM)
    anywhere = pl.BlockSpec(memory_space=pl.ANY)
    dma = pltpu.SemaphoreType.DMA
    shape = jax.ShapeDtypeStruct
    vmem = pltpu.VMEM
    gain_enc = gain_enc.reshape(width // 128, 128)
    tokens_all = vmem((n_mp, seq_len, feat), BF16)
    half_all = vmem((n_mp, seq_len // 2, feat), BF16)
    rows_all = vmem((n_mp, readings, share, width), BF16)
    slots = vmem((n_dp, share, width), BF16)
    local = vmem((seq_len, head_cols), BF16)
    memory = vmem((readings, NLEN, head_cols), BF16)
    rows_x = vmem((n_x, readings, share, width), BF16)
    tokens_x = vmem((n_x, seq_len, feat), BF16)
    mixed, squares, rows = pl.pallas_call(
        functools.partial(layer_kernel, n_dp, n_mp),
        out_shape=(
            shape((seq_len, feat), BF16),
            shape((8, seq_len), F32),
            shape((own_rows, share, width), BF16),
        ),
        in_specs=[anywhere] * 2 + [block] + [anywhere] * 2 + [block] * 2 + [anywhere] * 2 + [smem],
        out_specs=(block,) * 3,
        scratch_shapes=[
            tokens_all, half_all, half_all, rows_all, tokens_all,
            vmem((n_mp, feat, head_cols), BF16),
            vmem(w_out.shape, BF16),
            vmem(w_key.shape, BF16),
            vmem(w_value.shape, BF16),
            vmem((own_rows, share, width), F32),
            slots, slots,
            vmem((readings, 128), jnp.int32),
            vmem((n_dp, readings, 128), jnp.int32),
            local, local, memory, memory,
            vmem((blocks, head_cols // HD, BLOCK, NEIGH * NLEN), F32),
            vmem((seq_len, head_cols), F32),
            local, memory, memory,
            rows_all, tokens_all,
            rows_x, rows_x, rows_x, tokens_x, tokens_x, tokens_x,
            vmem((readings, share, width), BF16),
            slots, slots,
            vmem((8, seq_len), F32),
            vmem((n_mp, 8, seq_len), F32),
            dma((7,)),
            dma((4, 2 * n_x)), dma((4, 2 * n_x)),
            dma((n_dp,)), dma((n_dp,)), dma((n_dp,)), dma((n_dp,)),
            dma((3, n_x)), dma((3, n_x)), dma((3, n_x)), dma((3, n_x)),
            dma((2, n_dp)), dma((2, n_dp)), dma((n_mp,)), dma((n_mp,)),
        ],
        compiler_params=pltpu.CompilerParams(
            collective_id=0, has_side_effects=True, vmem_limit_bytes=60 * 1024 * 1024
        ),
        name="layer",
    )(
        tokens, cotangent, gain_dec.reshape(n_mp, 1, feat), w_query.reshape(n_mp, feat, head_cols),
        w_out, encodings, gain_enc, w_key, w_value, neighbour_ids.T,
    )
    return pl.pallas_call(
        functools.partial(finish_kernel, n_mp),
        out_shape=(
            shape((seq_len, feat), BF16),
            shape((seq_len, feat), BF16),
            shape((own_rows, share, width), BF16),
        ),
        in_specs=[block] * 6,
        out_specs=(block,) * 3,
        name="finish",
    )(mixed, squares, rows, encodings, gain_enc, gain_post.reshape(n_mp, 1, feat))


def solution(mesh):
    in_specs = (
        P("dp", "mp"),
        P("dp", "mp"),
        P(),
        P(None, "mp"),
        P("mp", None),
        P("dp", "mp", None),
        P(),
        P(None, "mp"),
        P(None, "mp"),
        P(),
        P("dp", None),
    )
    out_specs = (P("dp", "mp"), P("dp", "mp"), P("dp", "mp", None))
    return jax.shard_map(shards, mesh=mesh, in_specs=in_specs, out_specs=out_specs, check_vma=False)
```
